512 devices in a mesh: node: 32 (over z, core), feat: 16 (over x, y).
Axes of the slice: x: 4, y: 4, z: 16, core: 2. Of those that a mesh axis runs over, the one named last changes fastest.
Arguments:
- features: bfloat16 [65536, 768], P('node', 'feat'), may hold values from -6 to 6
- weight: bfloat16 [768, 512], P('feat'), may hold values from -0.21875 to 0.21875
- bias: float32 [512], replicated, may hold values from -3 to 3
- tile_src: int32 [512, 32], P(('node', 'feat')), may hold values from 0 to 511, as said below
- tile_count: int32 [512], P(('node', 'feat')), may hold values from 2 to 32, as said below
- tile_vals: bfloat16 [512, 32, 128, 128], P(('node', 'feat')), may hold values from -0.125 to 0.125
Outputs:
- activated: bfloat16 [65536, 512], P(('node', 'feat'))
The draws below stay inside these ranges and needn't reach their ends.
Inputs may be any that keep to these rules, and one draw needn't show every extreme that they name: Block b of hidden belongs to node partition b // 16. In every row of tile_src the live slots (and all slots) name at most 2 blocks of any one node partition, and one partition supplies exactly 2 live slots in every row. `tile_count`: counts are uneven across destination blocks; some block is full in every draw.
All inputs are finite; a program needn't handle non-finite values.
Results may differ from the reference program's by a relative error of at most 0.0045.
Values may be sent and summed in bfloat16 or wider, within the bound.
A program may use at most 64 MiB of HBM per device.

```python
import jax
import jax.numpy as jnp
from jax import lax

D_IN = 768
HID = 512
BLK = 128
TILES = 32
CAP = 2
BLOCKS = 512
NODES = 65536
N_NODE = 32
N_FEAT = 16


def draw_tile_src(key, part):
    key = jax.random.fold_in(key, 11)

    def one_row(row_key):
        key_first, key_order, key_inside = jax.random.split(row_key, 3)
        first = jax.random.randint(key_first, (), 0, N_NODE).astype(jnp.int32)
        others = (jnp.arange(N_NODE * CAP - CAP).astype(jnp.int32) // CAP + first + 1) % N_NODE
        others = jax.random.permutation(key_order, others).astype(jnp.int32)
        leading = jnp.zeros((CAP,), jnp.int32) + first
        owners = jnp.concatenate([leading, others])[:TILES]
        inside = jax.random.randint(key_inside, (TILES,), 0, N_FEAT).astype(jnp.int32)
        return (owners * N_FEAT + inside).astype(jnp.int32)
    return jax.vmap(one_row)(jax.random.split(key, BLOCKS))


def draw_tile_count(key, part):
    key = jax.random.fold_in(key, 12)
    key_one, key_two, key_full = jax.random.split(key, 3)
    first = jax.random.randint(key_one, (BLOCKS,), CAP, TILES + 1)
    second = jax.random.randint(key_two, (BLOCKS,), CAP, TILES + 1)
    counts = jnp.minimum(first, second).astype(jnp.int32)
    fullest = jax.random.randint(key_full, (), 0, BLOCKS)
    counts = jnp.where(jnp.arange(BLOCKS) == fullest, TILES, counts)
    return counts.astype(jnp.int32)


def shard_levels(rng, dims, pieces, low, largest):
    def one(dim, shards_of):
        heights = jax.random.uniform(jax.random.fold_in(jax.random.fold_in(rng, 6), dim), (shards_of,), jnp.float32, low / len(pieces), largest / len(pieces))
        return jnp.repeat(jnp.exp(heights), dims[dim] // shards_of).reshape((-1,) + (1,) * (len(dims) - dim - 1))

    gain = one(*pieces[0])
    for cut in pieces[1:]:
        gain = gain * one(*cut)
    return gain


def centred(stream_key, shape, scale, bound, cuts=(), dtype=jnp.bfloat16):
    values = scale * jax.random.normal(stream_key, shape, jnp.float32)
    if cuts:
        values = values * shard_levels(stream_key, shape, cuts, -0.22, 0.18)
    return jnp.clip(values, -bound, bound).astype(dtype)


def setup_inputs(seed: int = 0) -> dict:
    splits = jax.random.split(jax.random.key(seed), 7)
    return {
        "features": centred(splits[0], (NODES, D_IN), 1.0, 6.0, ((0, 32), (1, 16))),
        "weight": centred(splits[1], (D_IN, HID), D_IN ** -0.5, 0.21875, ((0, 16),)),
        "bias": centred(splits[2], (HID,), 0.5, 3.0, (), jnp.float32),
        "tile_src": draw_tile_src(jax.random.fold_in(splits[6], 71), 0),
        "tile_count": draw_tile_count(jax.random.fold_in(splits[6], 71), 0),
        "tile_vals": centred(splits[5], (BLOCKS, TILES, BLK, BLK), (BLK * TILES // 2) ** -0.5, 0.125, ((0, 512),)),
    }


def reference(features, weight, bias, tile_src, tile_count, tile_vals):
    hidden = jnp.dot(features, weight, preferred_element_type=jnp.float32).astype(jnp.bfloat16)
    blocks = hidden.reshape(BLOCKS, BLK, HID)

    def one_block(items):
        sources, count, values = items
        alive = jnp.arange(TILES) < count
        picked = blocks[sources].astype(jnp.float32)
        live_vals = jnp.where(alive[:, None, None], values.astype(jnp.float32), jnp.zeros((), jnp.float32))
        summed = jnp.einsum("tij,tjh->ih", live_vals, picked)
        return jax.nn.relu(summed + bias).astype(jnp.bfloat16)

    result = lax.map(one_block, (tile_src, tile_count, tile_vals))
    return result.reshape(NODES, HID)
```

```python
import jax
import jax.numpy as jnp
from jax import lax
from jax.experimental import pallas as pl
from jax.experimental.pallas import tpu as pltpu
from jax.sharding import PartitionSpec as P

MESH = pl.DeviceIdType.MESH
NX, NY, NZ = 4, 4, 16
BLK = 128
COLS = 64
GROUP = 2 * NX
PART = 5
SHARD = 8
HALF = 3
BLOCKS = NZ * NY * SHARD
SLOTS = 32
UNROLL = 8


def kernel(
    ft, w, bias, src, cnt, tiles, out,
    xbuf, wbuf, hb, stage, tbuf, sv, ss, bt, obuf, rbuf,
    x_sem, w_sem, s_sem, ss_sem, t_sem, local_sem, h_sem, ry_sem, pz_sem, rz_sem, py_sem, pf_sem, o_sem,
):
    n = lax.axis_index("node")
    f = lax.axis_index("feat")
    z, c = lax.div(n, 2), lax.rem(n, 2)
    x, y = lax.div(f, NY), lax.rem(f, NY)
    me = x * 2 + c

    def at(xx, yy, zz, cc):
        return (zz * 2 + cc, xx * NY + yy)

    def up(value, size, by=1):
        return lax.rem(value + by, size)

    def down(value, size, by=1):
        return lax.rem(value + size - by, size)

    def remote(source, target, sems, index, device):
        return pltpu.make_async_remote_copy(
            src_ref=source, dst_ref=target, send_sem=sems.at[(0,) + index], recv_sem=sems.at[(1,) + index],
            device_id=device, device_id_type=MESH,
        )

    sibling = at(x, y, z, 1 - c)
    right, left = at(up(x, NX), y, z, c), at(down(x, NX), y, z, c)
    front, back = at(x, up(y, NY), z, c), at(x, down(y, NY), z, c)
    above, below = at(x, y, up(z, NZ), c), at(x, y, down(z, NZ), c)

    def group_peer(i):
        other = lax.rem(me + i, GROUP)
        return other, at(lax.div(other, 2), y, z, lax.rem(other, 2))

    barrier = pltpu.get_barrier_semaphore()

    @pl.loop(1, NX * NY)
    def _(i):
        pl.semaphore_signal(barrier, inc=1, device_id=(n, lax.rem(f + i, NX * NY)), device_id_type=MESH)

    for i in range(1, NX):
        pl.semaphore_signal(barrier, inc=1, device_id=at(up(x, NX, i), y, z, 1 - c), device_id_type=MESH)
    for device in (sibling, above, below):
        pl.semaphore_signal(barrier, inc=1, device_id=device, device_id_type=MESH)

    s = src[...]
    zz, rest = lax.shift_right_logical(s, 5), s & 31
    cc, ff = lax.shift_right_logical(rest, 4), rest & 15
    place = (zz * NY + lax.shift_right_logical(ff, 2)) * SHARD + cc * 4 + (ff & 3)
    alive = lax.broadcasted_iota(jnp.int32, s.shape, 1) < cnt[0]
    sv[me] = jnp.zeros((8, 128), jnp.int32)
    sv[me, 0:1, 0:SLOTS] = jnp.where(alive, place, BLOCKS)
    hb[BLOCKS] = jnp.zeros((COLS, BLK), jnp.bfloat16)
    bt[...] = jnp.broadcast_to(bias[pl.ds(x, 1), :], (128, 128)).T

    pl.semaphore_wait(barrier, NX * NY - 1 + NX - 1 + 3)

    def x_copy(i):
        peer = lax.rem(f + i, NX * NY)
        return remote(ft.at[lax.rem(peer, NY)], xbuf.at[f], x_sem, (i - 1,), (n, peer))

    def w_copy(i):
        peer = lax.rem(f + i, NX * NY)
        columns = pl.ds(pl.multiple_of(lax.div(peer, NY) * 128, 128), 128)
        return remote(w.at[:, columns], wbuf.at[f], w_sem, (i - 1,), (n, peer))

    @pl.loop(1, NX * NY)
    def _(i):
        x_copy(i).start()
        w_copy(i).start()

    xbuf[f] = ft[y]
    wbuf[f] = w[:, pl.ds(pl.multiple_of(x * 128, 128), 128)]

    def s_copy(i):
        _, device = group_peer(i)
        return remote(sv.at[me], sv.at[me], s_sem, (i - 1,), device)

    for i in range(1, GROUP):
        s_copy(i).start()

    @pl.loop(1, NX * NY)
    def _(i):
        x_copy(i).wait_recv()
        w_copy(i).wait_recv()

    own = tiles.at[0]
    low, high = pl.ds(0, SLOTS // 2), pl.ds(SLOTS // 2, SLOTS // 2)
    keep = pltpu.make_async_copy(own, tbuf.at[me], local_sem.at[0])
    keep.start()
    t_low_right = remote(own.at[low], tbuf.at[me, low], t_sem, (0,), right)
    t_high_left = remote(own.at[high], tbuf.at[me, high], t_sem, (1,), left)
    t_high_right = remote(own.at[high], tbuf.at[me, high], t_sem, (2,), right)
    t_low_left = remote(own.at[low], tbuf.at[me, low], t_sem, (3,), left)
    t_own_sibling = remote(own, tbuf.at[me], t_sem, (4,), sibling)
    for copy in (t_low_right, t_high_left, t_high_right, t_low_left, t_own_sibling):
        copy.start()
    from_left, from_right, from_far = (down(x, NX) * 2 + c, up(x, NX) * 2 + c, up(x, NX, 2) * 2 + c)
    t_pass_right = remote(tbuf.at[from_left, low], tbuf.at[from_left, low], t_sem, (5,), right)
    t_pass_left = remote(tbuf.at[from_right, high], tbuf.at[from_right, high], t_sem, (6,), left)
    t_sibling = [
        remote(tbuf.at[e], tbuf.at[e], t_sem, (7 + j,), sibling)
        for j, e in enumerate((from_left, from_right, from_far))
    ]

    ht = lax.dot_general(
        wbuf[...].reshape(NX * NY * 48, 128), xbuf[...].reshape(NX * NY * 48, 512),
        (((0,), (0,)), ((), ())), preferred_element_type=jnp.float32,
    ).astype(jnp.bfloat16)
    mine = jnp.where(c == 0, ht[:COLS], ht[COLS:])
    other = jnp.where(c == 0, ht[COLS:], ht[:COLS])
    place_of = lambda zz, yy: (zz * NY + yy) * SHARD
    base = place_of(z, y) + c * 4
    for k in range(4):
        stage[k] = other[:, k * BLK : (k + 1) * BLK]
    h_copy = remote(stage, hb.at[pl.ds(base, 4)], h_sem, (0,), sibling)
    h_copy.start()
    for k in range(4):
        hb[base + k] = mine[:, k * BLK : (k + 1) * BLK]
    h_copy.wait_recv()

    def blocks(zz, yy, first, count):
        return hb.at[pl.ds(place_of(zz, yy) + first, count)]

    def ry_copy(j):
        ref = blocks(z, y, PART, SHARD - PART)
        return remote(ref, ref, ry_sem, (j - 1,), at(x, up(y, NY, j), z, c))

    def pz_copy(zz, step, direction, first=0, count=PART):
        ref = blocks(zz, y, first, count)
        return remote(ref, ref, pz_sem, (direction, step), (above, below)[direction])

    hz = hb.at[pl.ds(0, BLOCKS)].reshape(NZ, NY, SHARD, COLS, BLK)

    def rz_copy(zz, step, direction, first=0, count=NY):
        ref = hz.at[zz, pl.ds(first, count), pl.ds(PART, SHARD - PART)]
        return remote(ref, ref, rz_sem, (direction, step), (above, below)[direction])

    def py_copy(zz, yy, direction):
        ref = blocks(zz, yy, 0, PART)
        return remote(ref, ref, py_sem, (direction, zz), (front, back)[direction])

    def pf_copy(zz, yy, direction):
        ref = blocks(zz, yy, *((0, HALF), (HALF, PART - HALF))[direction])
        return remote(ref, ref, pf_sem, (direction, zz), (front, back)[direction])

    far = NZ // 2
    pz_copy(z, 0, 0).start()
    pz_copy(z, 0, 1).start()
    for j in range(1, NY):
        ry_copy(j).start()
    py_copy(z, y, 0).start()
    py_copy(z, y, 1).start()
    for j in range(1, NY):
        ry_copy(j).wait_recv()
    rz_copy(z, 0, 0).start()
    rz_copy(z, 0, 1).start()

    def p_arrived(step):
        lower, upper = down(z, NZ, step), up(z, NZ, step)
        pz_copy(lower, step - 1, 0).wait_recv()
        pz_copy(upper, step - 1, 1).wait_recv()
        return lower, upper

    @pl.loop(1, far - 1)
    def _(step):
        lower, upper = p_arrived(step)
        pz_copy(lower, step, 0).start()
        pz_copy(upper, step, 1).start()
        for zz in (lower, upper):
            py_copy(zz, y, 0).start()
            py_copy(zz, y, 1).start()

    lower, upper = p_arrived(far - 1)
    pz_last = (
        pz_copy(lower, far - 1, 0, 0, HALF),
        pz_copy(upper, far - 1, 1, HALF, PART - HALF),
    )
    for copy in pz_last:
        copy.start()
    for zz in (lower, upper):
        py_copy(zz, y, 0).start()
        py_copy(zz, y, 1).start()
    opposite = up(z, NZ, far)
    pz_copy(opposite, far - 1, 0, 0, HALF).wait_recv()
    pz_copy(opposite, far - 1, 1, HALF, PART - HALF).wait_recv()
    py_copy(opposite, y, 0).start()
    py_copy(opposite, y, 1).start()

    def pass_on(zz):
        py_copy(zz, down(y, NY), 0).wait_recv()
        pf_copy(zz, down(y, NY), 0).start()
        py_copy(zz, up(y, NY), 1).wait_recv()
        pf_copy(zz, up(y, NY), 1).start()

    def r_arrived(step):
        lower, upper = down(z, NZ, step), up(z, NZ, step)
        rz_copy(lower, step - 1, 0).wait_recv()
        rz_copy(upper, step - 1, 1).wait_recv()
        return lower, upper

    def r_step(step):
        lower, upper = r_arrived(step)
        rz_copy(lower, step, 0).start()
        rz_copy(upper, step, 1).start()
        return lower, upper

    pass_on(z)
    pass_on(opposite)

    def both(step):
        lower, upper = r_step(step)
        pass_on(lower)
        pass_on(upper)

    @pl.loop(1, 4)
    def _(step):
        both(step)

    t_low_right.wait_recv()
    t_pass_right.start()
    t_high_left.wait_recv()
    t_pass_left.start()
    t_high_right.wait_recv()
    t_sibling[0].start()
    t_low_left.wait_recv()
    t_sibling[1].start()

    @pl.loop(4, far - 1)
    def _(step):
        both(step)

    lower, upper = r_arrived(far - 1)
    rz_last = (
        rz_copy(lower, far - 1, 0, 0, NY // 2),
        rz_copy(upper, far - 1, 1, NY // 2, NY // 2),
    )
    for copy in rz_last:
        copy.start()
    pass_on(lower)
    pass_on(upper)

    remote(tbuf.at[from_far, low], tbuf.at[from_far, low], t_sem, (5,), right).wait_recv()
    remote(tbuf.at[from_far, high], tbuf.at[from_far, high], t_sem, (6,), left).wait_recv()
    t_sibling[2].start()

    rz_copy(opposite, far - 1, 0, 0, NY // 2).wait_recv()
    rz_copy(opposite, far - 1, 1, NY // 2, NY // 2).wait_recv()

    @pl.loop(0, NZ)
    def _(zz):
        pf_copy(zz, up(y, NY, 2), 0).wait_recv()
        pf_copy(zz, up(y, NY, 2), 1).wait_recv()

    for i in range(1, GROUP):
        s_copy(i).wait_recv()
    places = pltpu.make_async_copy(sv, ss, ss_sem.at[0])
    places.start()
    keep.wait()
    t_own_sibling.wait_recv()
    for copy in t_sibling:
        copy.wait_recv()
    places.wait()

    def aggregate(e):
        total = jnp.zeros((COLS, BLK), jnp.float32)
        for first in range(0, SLOTS, UNROLL):
            slots = range(first, first + UNROLL)
            picked = jnp.concatenate([hb[ss[e, 0, t]] for t in slots], axis=1)
            values = jnp.concatenate([tbuf[e, t] for t in slots], axis=1)
            total += lax.dot_general(
                picked, values, (((1,), (1,)), ((), ())), preferred_element_type=jnp.float32
            )
        return jnp.maximum(total + bt[pl.ds(pl.multiple_of(c * COLS, COLS), COLS), :], 0.0).astype(jnp.bfloat16)

    def o_copy(i):
        _, device = group_peer(i)
        return remote(obuf.at[i], rbuf.at[me], o_sem, (i - 1,), device)

    @pl.loop(1, GROUP)
    def _(i):
        e, _ = group_peer(i)
        obuf[i] = aggregate(e)
        o_copy(i).start()

    rbuf[me] = aggregate(me)

    @pl.loop(1, NX * NY)
    def _(i):
        x_copy(i).wait_send()
        w_copy(i).wait_send()

    for i in range(1, GROUP):
        s_copy(i).wait_send()
    for copy in (t_low_right, t_high_left, t_high_right, t_low_left, t_own_sibling, t_pass_right, t_pass_left, h_copy):
        copy.wait_send()
    for copy in t_sibling + list(pz_last) + list(rz_last):
        copy.wait_send()
    for j in range(1, NY):
        ry_copy(j).wait_send()

    @pl.loop(0, far - 1)
    def _(step):
        for direction in range(2):
            pz_copy(z, step, direction).wait_send()
            rz_copy(z, step, direction).wait_send()

    @pl.loop(0, NZ)
    def _(zz):
        for direction in range(2):
            py_copy(zz, y, direction).wait_send()
            pf_copy(zz, y, direction).wait_send()

    @pl.loop(1, GROUP)
    def _(i):
        o_copy(i).wait_recv()

    out[...] = rbuf[...].reshape(GROUP * COLS, BLK)

    @pl.loop(1, GROUP)
    def _(i):
        o_copy(i).wait_send()


def shards(features, weight, bias, tile_src, tile_count, tile_vals):
    rows, depth = features.shape
    ft = features.reshape(NY, rows // NY, depth).transpose(0, 2, 1)
    vmem = pl.BlockSpec(memory_space=pltpu.VMEM)
    smem = pl.BlockSpec(memory_space=pltpu.SMEM)
    dma = pltpu.SemaphoreType.DMA
    bf16 = jnp.bfloat16
    transposed = pl.pallas_call(
        kernel,
        out_shape=jax.ShapeDtypeStruct((GROUP * COLS, BLK), bf16),
        in_specs=[vmem, vmem, vmem, vmem, smem, pl.BlockSpec(memory_space=pl.ANY)],
        out_specs=vmem,
        scratch_shapes=[
            pltpu.VMEM((NX * NY, depth, rows // NY), bf16),
            pltpu.VMEM((NX * NY, depth, 128), bf16),
            pltpu.VMEM((BLOCKS + 1, COLS, BLK), bf16),
            pltpu.VMEM((4, COLS, BLK), bf16),
            pltpu.VMEM((GROUP, SLOTS, BLK, BLK), bf16),
            pltpu.VMEM((GROUP, 8, 128), jnp.int32),
            pltpu.SMEM((GROUP, 8, 128), jnp.int32),
            pltpu.VMEM((128, 128), jnp.float32),
            pltpu.VMEM((GROUP, COLS, BLK), bf16),
            pltpu.VMEM((GROUP, COLS, BLK), bf16),
            dma((2, NX * NY - 1)),
            dma((2, NX * NY - 1)),
            dma((2, GROUP - 1)),
            dma((1,)),
            dma((2, 10)),
            dma((1,)),
            dma((2, 1)),
            dma((2, NY - 1)),
            dma((2, 2, NZ // 2)),
            dma((2, 2, NZ // 2)),
            dma((2, 2, NZ)),
            dma((2, 2, NZ)),
            dma((2, GROUP - 1)),
        ],
        compiler_params=pltpu.CompilerParams(
            collective_id=0, has_side_effects=True, vmem_limit_bytes=40 * 2**20
        ),
    )(ft, weight, bias.reshape(NX, 128), tile_src, tile_count, tile_vals)
    return transposed.T


def solution(mesh):
    placed = (
        P("node", "feat"),
        P("feat", None),
        P(),
        P(("node", "feat"), None),
        P(("node", "feat")),
        P(("node", "feat"), None, None, None),
    )
    return jax.shard_map(
        shards, mesh=mesh, in_specs=placed, out_specs=P(("node", "feat"), None), check_vma=False
    )
```

```python
import jax
import jax.numpy as jnp
from jax import lax
from jax.experimental import pallas as pl
from jax.experimental.pallas import tpu as pltpu
from jax.sharding import PartitionSpec as P

MESH = pl.DeviceIdType.MESH
NX, NY, NZ = 4, 4, 16
BLK = 128
COLS = 64
GROUP = 2 * NX
PART = 5
SHARD = 8
HALF = 3
BLOCKS = NZ * NY * SHARD
SLOTS = 32
UNROLL = 8


def kernel(
    ft, w, bias, src, cnt, tiles, out,
    xbuf, wbuf, hb, stage, tbuf, sv, ss, bt, obuf, rbuf,
    x_sem, w_sem, s_sem, ss_sem, t_sem, local_sem, h_sem, ry_sem, pz_sem, rz_sem, py_sem, pf_sem, o_sem,
):
    n = lax.axis_index("node")
    f = lax.axis_index("feat")
    z, c = lax.div(n, 2), lax.rem(n, 2)
    x, y = lax.div(f, NY), lax.rem(f, NY)
    me = x * 2 + c

    def at(xx, yy, zz, cc):
        return (zz * 2 + cc, xx * NY + yy)

    def up(value, size, by=1):
        return lax.rem(value + by, size)

    def down(value, size, by=1):
        return lax.rem(value + size - by, size)

    def remote(source, target, sems, index, device):
        return pltpu.make_async_remote_copy(
            src_ref=source, dst_ref=target, send_sem=sems.at[(0,) + index], recv_sem=sems.at[(1,) + index],
            device_id=device, device_id_type=MESH,
        )

    sibling = at(x, y, z, 1 - c)
    right, left = at(up(x, NX), y, z, c), at(down(x, NX), y, z, c)
    front, back = at(x, up(y, NY), z, c), at(x, down(y, NY), z, c)
    above, below = at(x, y, up(z, NZ), c), at(x, y, down(z, NZ), c)

    def group_peer(i):
        other = lax.rem(me + i, GROUP)
        return other, at(lax.div(other, 2), y, z, lax.rem(other, 2))

    barrier = pltpu.get_barrier_semaphore()

    @pl.loop(1, NX * NY)
    def _(i):
        pl.semaphore_signal(barrier, inc=1, device_id=(n, lax.rem(f + i, NX * NY)), device_id_type=MESH)

    for i in range(1, NX):
        pl.semaphore_signal(barrier, inc=1, device_id=at(up(x, NX, i), y, z, 1 - c), device_id_type=MESH)
    for device in (sibling, above, below):
        pl.semaphore_signal(barrier, inc=1, device_id=device, device_id_type=MESH)

    s = src[...]
    zz, rest = lax.shift_right_logical(s, 5), s & 31
    cc, ff = lax.shift_right_logical(rest, 4), rest & 15
    place = (zz * NY + lax.shift_right_logical(ff, 2)) * SHARD + cc * 4 + (ff & 3)
    alive = lax.broadcasted_iota(jnp.int32, s.shape, 1) < cnt[0]
    sv[me] = jnp.zeros((8, 128), jnp.int32)
    sv[me, 0:1, 0:SLOTS] = jnp.where(alive, place, BLOCKS)
    hb[BLOCKS] = jnp.zeros((COLS, BLK), jnp.bfloat16)
    bt[...] = jnp.broadcast_to(bias[pl.ds(x, 1), :], (128, 128)).T

    pl.semaphore_wait(barrier, NX * NY - 1 + NX - 1 + 3)

    def x_copy(i):
        peer = lax.rem(f + i, NX * NY)
        return remote(ft.at[lax.rem(peer, NY)], xbuf.at[f], x_sem, (i - 1,), (n, peer))

    def w_copy(i):
        peer = lax.rem(f + i, NX * NY)
        columns = pl.ds(pl.multiple_of(lax.div(peer, NY) * 128, 128), 128)
        return remote(w.at[:, columns], wbuf.at[f], w_sem, (i - 1,), (n, peer))

    @pl.loop(1, NX * NY)
    def _(i):
        x_copy(i).start()
        w_copy(i).start()

    xbuf[f] = ft[y]
    wbuf[f] = w[:, pl.ds(pl.multiple_of(x * 128, 128), 128)]

    def s_copy(i):
        _, device = group_peer(i)
        return remote(sv.at[me], sv.at[me], s_sem, (i - 1,), device)

    for i in range(1, GROUP):
        s_copy(i).start()

    @pl.loop(1, NX * NY)
    def _(i):
        x_copy(i).wait_recv()
        w_copy(i).wait_recv()

    own = tiles.at[0]
    low, high = pl.ds(0, SLOTS // 2), pl.ds(SLOTS // 2, SLOTS // 2)
    keep = pltpu.make_async_copy(own, tbuf.at[me], local_sem.at[0])
    keep.start()
    t_low_right = remote(own.at[low], tbuf.at[me, low], t_sem, (0,), right)
    t_high_left = remote(own.at[high], tbuf.at[me, high], t_sem, (1,), left)
    t_high_right = remote(own.at[high], tbuf.at[me, high], t_sem, (2,), right)
    t_low_left = remote(own.at[low], tbuf.at[me, low], t_sem, (3,), left)
    t_own_sibling = remote(own, tbuf.at[me], t_sem, (4,), sibling)
    for copy in (t_low_right, t_high_left, t_high_right, t_low_left, t_own_sibling):
        copy.start()
    from_left, from_right, from_far = (down(x, NX) * 2 + c, up(x, NX) * 2 + c, up(x, NX, 2) * 2 + c)
    t_pass_right = remote(tbuf.at[from_left, low], tbuf.at[from_left, low], t_sem, (5,), right)
    t_pass_left = remote(tbuf.at[from_right, high], tbuf.at[from_right, high], t_sem, (6,), left)
    t_sibling = [
        remote(tbuf.at[e], tbuf.at[e], t_sem, (7 + j,), sibling)
        for j, e in enumerate((from_left, from_right, from_far))
    ]

    ht = lax.dot_general(
        wbuf[...].reshape(NX * NY * 48, 128), xbuf[...].reshape(NX * NY * 48, 512),
        (((0,), (0,)), ((), ())), preferred_element_type=jnp.float32,
    ).astype(jnp.bfloat16)
    mine = jnp.where(c == 0, ht[:COLS], ht[COLS:])
    other = jnp.where(c == 0, ht[COLS:], ht[:COLS])
    place_of = lambda zz, yy: (zz * NY + yy) * SHARD
    base = place_of(z, y) + c * 4
    for k in range(4):
        stage[k] = other[:, k * BLK : (k + 1) * BLK]
    h_copy = remote(stage, hb.at[pl.ds(base, 4)], h_sem, (0,), sibling)
    h_copy.start()
    for k in range(4):
        hb[base + k] = mine[:, k * BLK : (k + 1) * BLK]
    h_copy.wait_recv()

    def blocks(zz, yy, first, count):
        return hb.at[pl.ds(place_of(zz, yy) + first, count)]

    def ry_copy(j):
        ref = blocks(z, y, PART, SHARD - PART)
        return remote(ref, ref, ry_sem, (j - 1,), at(x, up(y, NY, j), z, c))

    def pz_copy(zz, step, direction, first=0, count=PART):
        ref = blocks(zz, y, first, count)
        return remote(ref, ref, pz_sem, (direction, step), (above, below)[direction])

    hz = hb.at[pl.ds(0, BLOCKS)].reshape(NZ, NY, SHARD, COLS, BLK)

    def rz_copy(zz, step, direction, part):
        ref = hz.at[zz, pl.ds(part * (NY // 2), NY // 2), pl.ds(PART, SHARD - PART)]
        return remote(ref, ref, rz_sem, (direction, part, step), (above, below)[direction])

    def py_copy(zz, yy, direction):
        ref = blocks(zz, yy, 0, PART)
        return remote(ref, ref, py_sem, (direction, zz), (front, back)[direction])

    def pf_copy(zz, yy, direction):
        ref = blocks(zz, yy, *((0, HALF), (HALF, PART - HALF))[direction])
        return remote(ref, ref, pf_sem, (direction, zz), (front, back)[direction])

    far = NZ // 2
    pz_copy(z, 0, 0).start()
    pz_copy(z, 0, 1).start()
    for j in range(1, NY):
        ry_copy(j).start()
    py_copy(z, y, 0).start()
    py_copy(z, y, 1).start()
    for j in range(1, NY):
        ry_copy(j).wait_recv()
    for part in range(2):
        rz_copy(z, 0, 0, part).start()
        rz_copy(z, 0, 1, part).start()

    def spread(zz):
        py_copy(zz, y, 0).start()
        py_copy(zz, y, 1).start()

    def pass_on(zz):
        py_copy(zz, down(y, NY), 0).wait_recv()
        pf_copy(zz, down(y, NY), 0).start()
        py_copy(zz, up(y, NY), 1).wait_recv()
        pf_copy(zz, up(y, NY), 1).start()

    def ring_step(step):
        lower, upper = down(z, NZ, step), up(z, NZ, step)
        pz_copy(lower, step - 1, 0).wait_recv()
        pz_copy(lower, step, 0).start()
        pz_copy(upper, step - 1, 1).wait_recv()
        pz_copy(upper, step, 1).start()
        spread(lower)
        spread(upper)
        for part in range(2):
            rz_copy(lower, step - 1, 0, part).wait_recv()
            rz_copy(lower, step, 0, part).start()
            rz_copy(upper, step - 1, 1, part).wait_recv()
            rz_copy(upper, step, 1, part).start()

    ring_step(1)
    pass_on(z)

    @pl.loop(2, far - 1)
    def _(step):
        ring_step(step)
        pass_on(down(z, NZ, step - 1))
        pass_on(up(z, NZ, step - 1))

        @pl.when(step == 4)
        def _():
            t_low_right.wait_recv()
            t_pass_right.start()
            t_high_left.wait_recv()
            t_pass_left.start()

        @pl.when(step == 5)
        def _():
            t_high_right.wait_recv()
            t_sibling[0].start()
            t_low_left.wait_recv()
            t_sibling[1].start()

    lower, upper, opposite = down(z, NZ, far - 1), up(z, NZ, far - 1), up(z, NZ, far)
    pz_last = (
        pz_copy(lower, far - 1, 0, 0, HALF),
        pz_copy(upper, far - 1, 1, HALF, PART - HALF),
    )
    rz_last = (rz_copy(lower, far - 1, 0, 0), rz_copy(upper, far - 1, 1, 1))
    pz_copy(lower, far - 2, 0).wait_recv()
    pz_last[0].start()
    pz_copy(upper, far - 2, 1).wait_recv()
    pz_last[1].start()
    spread(lower)
    spread(upper)
    rz_copy(lower, far - 2, 0, 0).wait_recv()
    rz_last[0].start()
    rz_copy(upper, far - 2, 1, 1).wait_recv()
    rz_last[1].start()
    rz_copy(lower, far - 2, 0, 1).wait_recv()
    rz_copy(upper, far - 2, 1, 0).wait_recv()
    pass_on(down(z, NZ, far - 2))
    pass_on(up(z, NZ, far - 2))
    pz_copy(opposite, far - 1, 0, 0, HALF).wait_recv()
    pz_copy(opposite, far - 1, 1, HALF, PART - HALF).wait_recv()
    spread(opposite)
    pass_on(lower)
    pass_on(upper)

    remote(tbuf.at[from_far, low], tbuf.at[from_far, low], t_sem, (5,), right).wait_recv()
    remote(tbuf.at[from_far, high], tbuf.at[from_far, high], t_sem, (6,), left).wait_recv()
    t_sibling[2].start()

    rz_copy(opposite, far - 1, 0, 0).wait_recv()
    rz_copy(opposite, far - 1, 1, 1).wait_recv()
    pass_on(opposite)

    @pl.loop(0, NZ)
    def _(zz):
        pf_copy(zz, up(y, NY, 2), 0).wait_recv()
        pf_copy(zz, up(y, NY, 2), 1).wait_recv()

    for i in range(1, GROUP):
        s_copy(i).wait_recv()
    places = pltpu.make_async_copy(sv, ss, ss_sem.at[0])
    places.start()
    keep.wait()
    t_own_sibling.wait_recv()
    for copy in t_sibling:
        copy.wait_recv()
    places.wait()

    def aggregate(e):
        total = jnp.zeros((COLS, BLK), jnp.float32)
        for first in range(0, SLOTS, UNROLL):
            slots = range(first, first + UNROLL)
            picked = jnp.concatenate([hb[ss[e, 0, t]] for t in slots], axis=1)
            values = jnp.concatenate([tbuf[e, t] for t in slots], axis=1)
            total += lax.dot_general(
                picked, values, (((1,), (1,)), ((), ())), preferred_element_type=jnp.float32
            )
        return jnp.maximum(total + bt[pl.ds(pl.multiple_of(c * COLS, COLS), COLS), :], 0.0).astype(jnp.bfloat16)

    def o_copy(i):
        _, device = group_peer(i)
        return remote(obuf.at[i], rbuf.at[me], o_sem, (i - 1,), device)

    @pl.loop(1, GROUP)
    def _(i):
        e, _ = group_peer(i)
        obuf[i] = aggregate(e)
        o_copy(i).start()

    rbuf[me] = aggregate(me)

    @pl.loop(1, NX * NY)
    def _(i):
        x_copy(i).wait_send()
        w_copy(i).wait_send()

    for i in range(1, GROUP):
        s_copy(i).wait_send()
    for copy in (t_low_right, t_high_left, t_high_right, t_low_left, t_own_sibling, t_pass_right, t_pass_left, h_copy):
        copy.wait_send()
    for copy in t_sibling + list(pz_last) + list(rz_last):
        copy.wait_send()
    for j in range(1, NY):
        ry_copy(j).wait_send()

    @pl.loop(0, far - 1)
    def _(step):
        for direction in range(2):
            pz_copy(z, step, direction).wait_send()
            rz_copy(z, step, direction, 0).wait_send()
            rz_copy(z, step, direction, 1).wait_send()

    @pl.loop(0, NZ)
    def _(zz):
        for direction in range(2):
            py_copy(zz, y, direction).wait_send()
            pf_copy(zz, y, direction).wait_send()

    @pl.loop(1, GROUP)
    def _(i):
        o_copy(i).wait_recv()

    out[...] = rbuf[...].reshape(GROUP * COLS, BLK)

    @pl.loop(1, GROUP)
    def _(i):
        o_copy(i).wait_send()


def shards(features, weight, bias, tile_src, tile_count, tile_vals):
    rows, depth = features.shape
    ft = features.reshape(NY, rows // NY, depth).transpose(0, 2, 1)
    vmem = pl.BlockSpec(memory_space=pltpu.VMEM)
    smem = pl.BlockSpec(memory_space=pltpu.SMEM)
    dma = pltpu.SemaphoreType.DMA
    bf16 = jnp.bfloat16
    transposed = pl.pallas_call(
        kernel,
        out_shape=jax.ShapeDtypeStruct((GROUP * COLS, BLK), bf16),
        in_specs=[vmem, vmem, vmem, vmem, smem, pl.BlockSpec(memory_space=pl.ANY)],
        out_specs=vmem,
        scratch_shapes=[
            pltpu.VMEM((NX * NY, depth, rows // NY), bf16),
            pltpu.VMEM((NX * NY, depth, 128), bf16),
            pltpu.VMEM((BLOCKS + 1, COLS, BLK), bf16),
            pltpu.VMEM((4, COLS, BLK), bf16),
            pltpu.VMEM((GROUP, SLOTS, BLK, BLK), bf16),
            pltpu.VMEM((GROUP, 8, 128), jnp.int32),
            pltpu.SMEM((GROUP, 8, 128), jnp.int32),
            pltpu.VMEM((128, 128), jnp.float32),
            pltpu.VMEM((GROUP, COLS, BLK), bf16),
            pltpu.VMEM((GROUP, COLS, BLK), bf16),
            dma((2, NX * NY - 1)),
            dma((2, NX * NY - 1)),
            dma((2, GROUP - 1)),
            dma((1,)),
            dma((2, 10)),
            dma((1,)),
            dma((2, 1)),
            dma((2, NY - 1)),
            dma((2, 2, NZ // 2)),
            dma((2, 2, 2, NZ // 2)),
            dma((2, 2, NZ)),
            dma((2, 2, NZ)),
            dma((2, GROUP - 1)),
        ],
        compiler_params=pltpu.CompilerParams(
            collective_id=0, has_side_effects=True, vmem_limit_bytes=40 * 2**20
        ),
    )(ft, weight, bias.reshape(NX, 128), tile_src, tile_count, tile_vals)
    return transposed.T


def solution(mesh):
    placed = (
        P("node", "feat"),
        P("feat", None),
        P(),
        P(("node", "feat"), None),
        P(("node", "feat")),
        P(("node", "feat"), None, None, None),
    )
    return jax.shard_map(
        shards, mesh=mesh, in_specs=placed, out_specs=P(("node", "feat"), None), check_vma=False
    )
```

```python
import jax
import jax.numpy as jnp
from jax import lax
from jax.experimental import pallas as pl
from jax.experimental.pallas import tpu as pltpu
from jax.sharding import PartitionSpec as P

MESH = pl.DeviceIdType.MESH
NX, NY, NZ = 4, 4, 16
BLK = 128
COLS = 64
GROUP = 2 * NX
PART = 5
SHARD = 8
HALF = 3
BLOCKS = NZ * NY * SHARD
SLOTS = 32
UNROLL = 8
ROWS = 512
ORDER = (
    "R0 R1 P1 R2", "Y0 R3 R4 P2", "R5 Y1 R6 R7", "P3 R8 Y2 R9",
    "R10 P4 R11 R12", "Y3 R13 P5 T0", "R14 R15 Y4 R16", "P6 R17 R18 Y5",
    "R19 P7 T1 R20", "R21 R22 P8 R23", "R24 Y6 R25 R26", "Y7 R27 Y8 R28",
    "R30 R29 R31",
)
PLANE = (
    (2, 2), (2, 1), (1, 2), (2, 3), (3, 2), (1, 1), (3, 3), (1, 3), (3, 1), (2, 0), (0, 2), (1, 0), (3, 0), (0, 1), (0, 3),
)


def kernel(
    ft, w, bias, src, cnt, tiles, out,
    xbuf, wbuf, hb, stage, tbuf, sv, ss, bt, obuf, rbuf,
    bv, iv, x_sem, w_sem, s_sem, ss_sem, t_sem, local_sem, h_sem, ry_sem, pz_sem, rz_sem, py_sem, pf_sem, o_sem,
):
    n = lax.axis_index("node")
    f = lax.axis_index("feat")
    z, c = lax.div(n, 2), lax.rem(n, 2)
    x, y = lax.div(f, NY), lax.rem(f, NY)
    me = x * 2 + c

    def at(xx, yy, zz, cc):
        return (zz * 2 + cc, xx * NY + yy)

    def up(value, size, by=1):
        return lax.rem(value + by, size)

    def down(value, size, by=1):
        return lax.rem(value + size - by, size)

    def remote(source, target, sems, index, device):
        return pltpu.make_async_remote_copy(
            src_ref=source, dst_ref=target, send_sem=sems.at[(0,) + index], recv_sem=sems.at[(1,) + index],
            device_id=device, device_id_type=MESH,
        )

    sibling = at(x, y, z, 1 - c)
    right, left = at(up(x, NX), y, z, c), at(down(x, NX), y, z, c)
    front, back = at(x, up(y, NY), z, c), at(x, down(y, NY), z, c)
    above, below = at(x, y, up(z, NZ), c), at(x, y, down(z, NZ), c)

    def group_peer(i):
        dx, dc = lax.rem(1 + lax.div(i, 2), NX), 1 - lax.rem(i, 2)
        xx, cc = up(x, NX, dx), lax.rem(c + dc, 2)
        return xx * 2 + cc, at(xx, y, z, cc)

    def group_source(i):
        dx, dc = lax.rem(1 + lax.div(i, 2), NX), 1 - lax.rem(i, 2)
        return down(x, NX, dx) * 2 + lax.rem(c + dc, 2)

    barrier = pltpu.get_barrier_semaphore()

    @pl.loop(1, NX * NY)
    def _(i):
        pl.semaphore_signal(barrier, inc=1, device_id=(n, lax.rem(f + i, NX * NY)), device_id_type=MESH)

    for i in range(1, NX):
        pl.semaphore_signal(barrier, inc=1, device_id=at(up(x, NX, i), y, z, 1 - c), device_id_type=MESH)
    for device in (sibling, above, below):
        pl.semaphore_signal(barrier, inc=1, device_id=device, device_id_type=MESH)

    local = [
        pltpu.make_async_copy(source, target, local_sem.at[i])
        for i, (source, target) in enumerate((
            (tiles.at[0], tbuf.at[me]),
            (bias, bv),
            (src, iv),
            (ft.at[:, pl.ds(pl.multiple_of(y * ROWS, ROWS), ROWS)], xbuf.at[f]),
            (w.at[:, pl.ds(pl.multiple_of(x * 128, 128), 128)], wbuf.at[f]),
        ))
    ]
    for copy in local:
        copy.start()

    hb[BLOCKS] = jnp.zeros((COLS, BLK), jnp.bfloat16)
    local[1].wait()
    bt[...] = jnp.broadcast_to(bv[pl.ds(x, 1), :], (128, 128)).T
    local[2].wait()
    s = iv[...]
    zz, rest = lax.shift_right_logical(s, 5), s & 31
    cc, ff = lax.shift_right_logical(rest, 4), rest & 15
    place = (zz * NY + lax.shift_right_logical(ff, 2)) * SHARD + cc * 4 + (ff & 3)
    alive = lax.broadcasted_iota(jnp.int32, s.shape, 1) < cnt[0]
    sv[me] = jnp.zeros((8, 128), jnp.int32)
    sv[me, 0:1, 0:SLOTS] = jnp.where(alive, place, BLOCKS)

    pl.semaphore_wait(barrier, NX * NY - 1 + NX - 1 + 3)

    def plane_copies(i):
        dx, dy = PLANE[i]
        xx, yy = up(x, NX, dx), up(y, NY, dy)
        rows = pl.ds(pl.multiple_of(yy * ROWS, ROWS), ROWS)
        columns = pl.ds(pl.multiple_of(xx * 128, 128), 128)
        device = at(xx, yy, z, c)
        return (
            remote(ft.at[:, rows], xbuf.at[f], x_sem, (i,), device),
            remote(w.at[:, columns], wbuf.at[f], w_sem, (i,), device),
        )

    plane = [copy for i in range(len(PLANE)) for copy in plane_copies(i)]
    for copy in plane:
        copy.start()

    def s_copy(i):
        _, device = group_peer(i)
        return remote(sv.at[me], sv.at[me], s_sem, (i,), device)

    for i in range(GROUP - 1):
        s_copy(i).start()
    local[3].wait()
    local[4].wait()
    for copy in plane:
        copy.wait_recv()

    own = tiles.at[0]
    low, high = pl.ds(0, SLOTS // 2), pl.ds(SLOTS // 2, SLOTS // 2)
    t_low_right = remote(own.at[low], tbuf.at[me, low], t_sem, (0,), right)
    t_high_left = remote(own.at[high], tbuf.at[me, high], t_sem, (1,), left)
    t_high_right = remote(own.at[high], tbuf.at[me, high], t_sem, (2,), right)
    t_low_left = remote(own.at[low], tbuf.at[me, low], t_sem, (3,), left)
    t_own_sibling = remote(own, tbuf.at[me], t_sem, (4,), sibling)
    for copy in (t_low_right, t_high_left, t_high_right, t_low_left, t_own_sibling):
        copy.start()
    from_left, from_right, from_far = (down(x, NX) * 2 + c, up(x, NX) * 2 + c, up(x, NX, 2) * 2 + c)
    t_pass_right = remote(tbuf.at[from_left, low], tbuf.at[from_left, low], t_sem, (5,), right)
    t_pass_left = remote(tbuf.at[from_right, high], tbuf.at[from_right, high], t_sem, (6,), left)
    t_sibling = [
        remote(tbuf.at[e], tbuf.at[e], t_sem, (7 + j,), sibling)
        for j, e in enumerate((from_left, from_right, from_far))
    ]

    ht = lax.dot_general(
        wbuf[...].reshape(NX * NY * 48, 128), xbuf[...].reshape(NX * NY * 48, 512),
        (((0,), (0,)), ((), ())), preferred_element_type=jnp.float32,
    ).astype(jnp.bfloat16)
    mine = jnp.where(c == 0, ht[:COLS], ht[COLS:])
    other = jnp.where(c == 0, ht[COLS:], ht[:COLS])
    place_of = lambda zz, yy: (zz * NY + yy) * SHARD
    base = place_of(z, y) + c * 4
    for k in range(4):
        stage[k] = other[:, k * BLK : (k + 1) * BLK]
    h_copy = remote(stage, hb.at[pl.ds(base, 4)], h_sem, (0,), sibling)
    h_copy.start()
    for k in range(4):
        hb[base + k] = mine[:, k * BLK : (k + 1) * BLK]
    h_copy.wait_recv()

    def blocks(zz, yy, first, count):
        return hb.at[pl.ds(place_of(zz, yy) + first, count)]

    def ry_copy(j):
        ref = blocks(z, y, PART, SHARD - PART)
        return remote(ref, ref, ry_sem, (j - 1,), at(x, up(y, NY, j), z, c))

    def pz_copy(zz, step, direction, first=0, count=PART):
        ref = blocks(zz, y, first, count)
        return remote(ref, ref, pz_sem, (direction, step), (above, below)[direction])

    def rz_copy(step, j, direction):
        zz = down(z, NZ, step) if direction == 0 else up(z, NZ, step)
        ref = blocks(zz, down(y, NY, j), PART, SHARD - PART)
        return remote(ref, ref, rz_sem, (direction, j, step), (above, below)[direction])

    def py_copy(zz, yy, direction):
        ref = blocks(zz, yy, 0, PART)
        return remote(ref, ref, py_sem, (direction, zz), (front, back)[direction])

    def pf_copy(zz, yy, direction, first):
        ref = blocks(zz, yy, *((0, HALF) if direction == first else (HALF, PART - HALF)))
        return remote(ref, ref, pf_sem, (direction, zz), (front, back)[direction])

    far = NZ // 2
    lower = [down(z, NZ, step) for step in range(far + 1)]
    upper = [up(z, NZ, step) for step in range(far + 1)]

    def p_copies(step):
        if step < far - 1:
            return [pz_copy(lower[step], step, 0), pz_copy(upper[step], step, 1)]
        return [pz_copy(lower[step], step, 0, 0, HALF), pz_copy(upper[step], step, 1, HALF, PART - HALF)]

    def r_copies(step, j):
        return [rz_copy(step, j, direction) for direction in range(2) if step < far - 1 or j // 2 == direction]

    def places_at(step):
        return [(lower[step], 0)] if step in (0, far) else [(lower[step], 0), (upper[step], 1)]

    def spread(step):
        for zz, _ in places_at(step):
            for direction in range(2):
                py_copy(zz, y, direction).start()

    def p_step(step):
        sends = p_copies(step) if step < far else [None, None]
        for arrival, send in zip(p_copies(step - 1), sends):
            arrival.wait_recv()
            if send is not None:
                send.start()
        spread(step)

    def r_step(q):
        step, j = q // NY, q % NY
        if step == 0 and j > 0:
            ry_copy(j).wait_recv()
        if step > 0:
            for copy in r_copies(step - 1, j):
                copy.wait_recv()
        if step < far:
            for copy in r_copies(step, j):
                copy.start()

    def y_step(step):
        for zz, first in places_at(step):
            for direction, yy in ((0, down(y, NY)), (1, up(y, NY))):
                py_copy(zz, yy, direction).wait_recv()
                pf_copy(zz, yy, direction, first).start()

    def t_step(part):
        if part == 0:
            t_low_right.wait_recv()
            t_pass_right.start()
            t_high_left.wait_recv()
            t_pass_left.start()
        else:
            t_high_right.wait_recv()
            t_sibling[0].start()
            t_low_left.wait_recv()
            t_sibling[1].start()

    for j in range(1, NY):
        ry_copy(j).start()
    for copy in p_copies(0):
        copy.start()
    spread(0)
    steps = {"P": p_step, "R": r_step, "Y": y_step, "T": t_step}
    for entry in " ".join(ORDER).split():
        steps[entry[0]](int(entry[1:]))
    for j in range(NY):
        for copy in r_copies(far - 1, j):
            copy.wait_recv()

    remote(tbuf.at[from_far, low], tbuf.at[from_far, low], t_sem, (5,), right).wait_recv()
    remote(tbuf.at[from_far, high], tbuf.at[from_far, high], t_sem, (6,), left).wait_recv()
    t_sibling[2].start()
    for step in range(far + 1):
        for zz, first in places_at(step):
            for direction in range(2):
                pf_copy(zz, up(y, NY, 2), direction, first).wait_recv()

    for i in range(GROUP - 1):
        s_copy(i).wait_recv()
    places = pltpu.make_async_copy(sv, ss, ss_sem.at[0])
    places.start()
    local[0].wait()
    t_own_sibling.wait_recv()
    for copy in t_sibling:
        copy.wait_recv()
    places.wait()

    def aggregate(e):
        total = jnp.zeros((COLS, BLK), jnp.float32)
        for first in range(0, SLOTS, UNROLL):
            slots = range(first, first + UNROLL)
            picked = jnp.concatenate([hb[ss[e, 0, t]] for t in slots], axis=1)
            values = jnp.concatenate([tbuf[e, t] for t in slots], axis=1)
            total += lax.dot_general(
                picked, values, (((1,), (1,)), ((), ())), preferred_element_type=jnp.float32
            )
        return jnp.maximum(total + bt[pl.ds(pl.multiple_of(c * COLS, COLS), COLS), :], 0.0).astype(jnp.bfloat16)

    def o_copy(i):
        _, device = group_peer(i)
        return remote(obuf.at[i], rbuf.at[me], o_sem, (i,), device)

    @pl.loop(0, GROUP - 1)
    def _(i):
        e, _ = group_peer(i)
        obuf[i] = aggregate(e)
        o_copy(i).start()

    rbuf[me] = aggregate(me)

    for copy in plane:
        copy.wait_send()

    for i in range(GROUP - 1):
        s_copy(i).wait_send()
    for copy in (t_low_right, t_high_left, t_high_right, t_low_left, t_own_sibling, t_pass_right, t_pass_left, h_copy):
        copy.wait_send()
    for copy in t_sibling:
        copy.wait_send()
    for j in range(1, NY):
        ry_copy(j).wait_send()

    for step in range(far):
        for copy in p_copies(step):
            copy.wait_send()
        for j in range(NY):
            for copy in r_copies(step, j):
                copy.wait_send()
    for step in range(far + 1):
        for zz, first in places_at(step):
            for direction in range(2):
                py_copy(zz, y, direction).wait_send()
                pf_copy(zz, y, direction, first).wait_send()

    @pl.loop(0, GROUP - 1)
    def _(i):
        o_copy(i).wait_recv()

    out[...] = rbuf[...].reshape(GROUP * COLS, BLK)

    @pl.loop(0, GROUP - 1)
    def _(i):
        o_copy(i).wait_send()


def shards(features, weight, bias, tile_src, tile_count, tile_vals):
    rows, depth = features.shape
    vmem = pl.BlockSpec(memory_space=pltpu.VMEM)
    hbm = pl.BlockSpec(memory_space=pltpu.HBM)
    smem = pl.BlockSpec(memory_space=pltpu.SMEM)
    dma = pltpu.SemaphoreType.DMA
    bf16 = jnp.bfloat16
    transposed = pl.pallas_call(
        kernel,
        out_shape=jax.ShapeDtypeStruct((GROUP * COLS, BLK), bf16),
        in_specs=[hbm, hbm, hbm, hbm, smem, hbm],
        out_specs=vmem,
        scratch_shapes=[
            pltpu.VMEM((NX * NY, depth, rows // NY), bf16),
            pltpu.VMEM((NX * NY, depth, 128), bf16),
            pltpu.VMEM((BLOCKS + 1, COLS, BLK), bf16),
            pltpu.VMEM((4, COLS, BLK), bf16),
            pltpu.VMEM((GROUP, SLOTS, BLK, BLK), bf16),
            pltpu.VMEM((GROUP, 8, 128), jnp.int32),
            pltpu.SMEM((GROUP, 8, 128), jnp.int32),
            pltpu.VMEM((128, 128), jnp.float32),
            pltpu.VMEM((GROUP, COLS, BLK), bf16),
            pltpu.VMEM((GROUP, COLS, BLK), bf16),
            pltpu.VMEM((NX, 128), jnp.float32),
            pltpu.VMEM((1, SLOTS), jnp.int32),
            dma((2, NX * NY - 1)),
            dma((2, NX * NY - 1)),
            dma((2, GROUP - 1)),
            dma((1,)),
            dma((2, 10)),
            dma((5,)),
            dma((2, 1)),
            dma((2, NY - 1)),
            dma((2, 2, NZ // 2)),
            dma((2, 2, NY, NZ // 2)),
            dma((2, 2, NZ)),
            dma((2, 2, NZ)),
            dma((2, GROUP - 1)),
        ],
        compiler_params=pltpu.CompilerParams(
            collective_id=0, has_side_effects=True, vmem_limit_bytes=56 * 2**20
        ),
    )(features.T, weight, bias.reshape(NX, 128), tile_src, tile_count, tile_vals)
    return transposed.T


def solution(mesh):
    placed = (
        P("node", "feat"),
        P("feat", None),
        P(),
        P(("node", "feat"), None),
        P(("node", "feat")),
        P(("node", "feat"), None, None, None),
    )
    return jax.shard_map(
        shards, mesh=mesh, in_specs=placed, out_specs=P(("node", "feat"), None), check_vma=False
    )
```

```python
import jax
import jax.numpy as jnp
from jax import lax
from jax.experimental import pallas as pl
from jax.experimental.pallas import tpu as pltpu
from jax.sharding import PartitionSpec as P

MESH = pl.DeviceIdType.MESH
NX, NY, NZ = 4, 4, 16
BLK = 128
COLS = 64
GROUP = 2 * NX
PART = 5
SHARD = 8
HALF = 3
BLOCKS = NZ * NY * SHARD
SLOTS = 32
UNROLL = 8
ROWS = 512
ORDER = (
    "R0 R1 P1 R2", "Y0 R3 R4 P2", "R5 Y1 R6 R7", "P3 R8 Y2 R9",
    "R10 P4 R11 R12", "Y3 R13 P5 T0", "R14 R15 Y4 R16", "P6 R17 R18 Y5",
    "R19 P7 T1 R20", "R21 R22 P8 R23", "R24 Y6 R25 R26", "T2 Y7 R27 Y8",
    "R28 R30 R29 R31",
)
PLANE = (
    (2, 2), (2, 1), (1, 2), (2, 3), (3, 2), (1, 1), (3, 3), (1, 3), (3, 1), (2, 0), (0, 2), (1, 0), (3, 0), (0, 1), (0, 3),
)


def kernel(
    ft, w, bias, src, cnt, tiles, out,
    xbuf, wbuf, hb, stage, tbuf, sv, ss, bt, obuf, rbuf,
    bv, iv, x_sem, w_sem, v_sem, s_sem, ss_sem, t_sem, local_sem, h_sem, ry_sem, pz_sem, rz_sem, py_sem, pf_sem, o_sem,
):
    n = lax.axis_index("node")
    f = lax.axis_index("feat")
    z, c = lax.div(n, 2), lax.rem(n, 2)
    x, y = lax.div(f, NY), lax.rem(f, NY)
    me = x * 2 + c

    def at(xx, yy, zz, cc):
        return (zz * 2 + cc, xx * NY + yy)

    def up(value, size, by=1):
        return lax.rem(value + by, size)

    def down(value, size, by=1):
        return lax.rem(value + size - by, size)

    def remote(source, target, sems, index, device):
        return pltpu.make_async_remote_copy(
            src_ref=source, dst_ref=target, send_sem=sems.at[(0,) + index], recv_sem=sems.at[(1,) + index],
            device_id=device, device_id_type=MESH,
        )

    sibling = at(x, y, z, 1 - c)
    right, left = at(up(x, NX), y, z, c), at(down(x, NX), y, z, c)
    front, back = at(x, up(y, NY), z, c), at(x, down(y, NY), z, c)
    above, below = at(x, y, up(z, NZ), c), at(x, y, down(z, NZ), c)

    def group_peer(i):
        dx, dc = lax.rem(1 + lax.div(i, 2), NX), 1 - lax.rem(i, 2)
        xx, cc = up(x, NX, dx), lax.rem(c + dc, 2)
        return xx * 2 + cc, at(xx, y, z, cc)

    def group_source(i):
        dx, dc = lax.rem(1 + lax.div(i, 2), NX), 1 - lax.rem(i, 2)
        return down(x, NX, dx) * 2 + lax.rem(c + dc, 2)

    barrier = pltpu.get_barrier_semaphore()

    @pl.loop(1, NX * NY)
    def _(i):
        pl.semaphore_signal(barrier, inc=1, device_id=(n, lax.rem(f + i, NX * NY)), device_id_type=MESH)

    for i in range(1, NX):
        pl.semaphore_signal(barrier, inc=1, device_id=at(up(x, NX, i), y, z, 1 - c), device_id_type=MESH)
    for device in (sibling, above, below):
        pl.semaphore_signal(barrier, inc=1, device_id=device, device_id_type=MESH)

    local = [
        pltpu.make_async_copy(source, target, local_sem.at[i])
        for i, (source, target) in enumerate((
            (tiles.at[0], tbuf.at[me]),
            (bias, bv),
            (src, iv),
            (ft.at[:, pl.ds(pl.multiple_of(y * ROWS, ROWS), ROWS)], xbuf.at[f]),
            (w.at[:, pl.ds(pl.multiple_of(x * 128, 128), 128)], wbuf.at[f]),
        ))
    ]
    for copy in local:
        copy.start()

    pl.semaphore_wait(barrier, NX * NY - 1 + NX - 1 + 3)

    def plane_peer(i):
        dx, dy = PLANE[i]
        return up(x, NX, dx), up(y, NY, dy)

    def x_copy(i):
        xx, yy = plane_peer(i)
        rows = pl.ds(pl.multiple_of(yy * ROWS, ROWS), ROWS)
        return remote(ft.at[:, rows], xbuf.at[f], x_sem, (i,), at(xx, yy, z, c))

    def w_copy(i):
        xx, yy = plane_peer(i)
        columns = pl.ds(pl.multiple_of(xx * 128, 128), 128)
        return remote(w.at[:, columns], wbuf.at[f], w_sem, (i,), at(xx, yy, z, c))

    def w_shares(method):
        for core in range(2):

            @pl.when(c == core)
            def _():
                for i in range(core, len(PLANE), 2):
                    method(i)

    w_shares(lambda i: w_copy(i).start())
    x_plane = [x_copy(i) for i in range(len(PLANE))]
    for copy in x_plane:
        copy.start()

    hb[BLOCKS] = jnp.zeros((COLS, BLK), jnp.bfloat16)
    local[1].wait()
    bt[...] = jnp.broadcast_to(bv[pl.ds(x, 1), :], (128, 128)).T
    local[2].wait()
    s = iv[...]
    zz, rest = lax.shift_right_logical(s, 5), s & 31
    cc, ff = lax.shift_right_logical(rest, 4), rest & 15
    place = (zz * NY + lax.shift_right_logical(ff, 2)) * SHARD + cc * 4 + (ff & 3)
    alive = lax.broadcasted_iota(jnp.int32, s.shape, 1) < cnt[0]
    sv[me] = jnp.zeros((8, 128), jnp.int32)
    sv[me, 0:1, 0:SLOTS] = jnp.where(alive, place, BLOCKS)

    def s_copy(i):
        _, device = group_peer(i)
        return remote(sv.at[me], sv.at[me], s_sem, (i,), device)

    for i in range(GROUP - 1):
        s_copy(i).start()
    local[3].wait()
    local[4].wait()
    def hand_on(i):
        dx, dy = PLANE[i]
        ref = wbuf.at[down(x, NX, dx) * NY + down(y, NY, dy)]
        return remote(ref, ref, v_sem, (i,), sibling)

    def pass_weights(i):
        w_copy(i).wait_recv()
        hand_on(i).start()

    w_shares(pass_weights)
    for copy in x_plane:
        copy.wait_recv()
    for core in range(2):

        @pl.when(c == core)
        def _():
            for i in range(1 - core, len(PLANE), 2):
                hand_on(i).wait_recv()


    own = tiles.at[0]
    low, high = pl.ds(0, SLOTS // 2), pl.ds(SLOTS // 2, SLOTS // 2)
    t_low_right = remote(own.at[low], tbuf.at[me, low], t_sem, (0,), right)
    t_high_left = remote(own.at[high], tbuf.at[me, high], t_sem, (1,), left)
    t_high_right = remote(own.at[high], tbuf.at[me, high], t_sem, (2,), right)
    t_low_left = remote(own.at[low], tbuf.at[me, low], t_sem, (3,), left)
    t_own_sibling = remote(own, tbuf.at[me], t_sem, (4,), sibling)
    for copy in (t_low_right, t_high_left, t_high_right, t_low_left):
        copy.start()
    from_left, from_right, from_far = (down(x, NX) * 2 + c, up(x, NX) * 2 + c, up(x, NX, 2) * 2 + c)
    t_pass_right = remote(tbuf.at[from_left, low], tbuf.at[from_left, low], t_sem, (5,), right)
    t_pass_left = remote(tbuf.at[from_right, high], tbuf.at[from_right, high], t_sem, (6,), left)
    t_sibling = [
        remote(tbuf.at[e], tbuf.at[e], t_sem, (7 + j,), sibling)
        for j, e in enumerate((from_left, from_right, from_far))
    ]

    t_from_right = remote(tbuf.at[from_far, low], tbuf.at[from_far, low], t_sem, (5,), right)
    t_from_left = remote(tbuf.at[from_far, high], tbuf.at[from_far, high], t_sem, (6,), left)
    places = pltpu.make_async_copy(sv, ss, ss_sem.at[0])

    ht = lax.dot_general(
        wbuf[...].reshape(NX * NY * 48, 128), xbuf[...].reshape(NX * NY * 48, 512),
        (((0,), (0,)), ((), ())), preferred_element_type=jnp.float32,
    ).astype(jnp.bfloat16)
    mine = jnp.where(c == 0, ht[:COLS], ht[COLS:])
    other = jnp.where(c == 0, ht[COLS:], ht[:COLS])
    place_of = lambda zz, yy: (zz * NY + yy) * SHARD
    base = place_of(z, y) + c * 4
    for k in range(4):
        stage[k] = other[:, k * BLK : (k + 1) * BLK]
    h_copy = remote(stage, hb.at[pl.ds(base, 4)], h_sem, (0,), sibling)
    h_copy.start()
    t_own_sibling.start()
    for k in range(4):
        hb[base + k] = mine[:, k * BLK : (k + 1) * BLK]
    h_copy.wait_recv()

    def blocks(zz, yy, first, count):
        return hb.at[pl.ds(place_of(zz, yy) + first, count)]

    def ry_copy(j):
        ref = blocks(z, y, PART, SHARD - PART)
        return remote(ref, ref, ry_sem, (j - 1,), at(x, up(y, NY, j), z, c))

    def pz_copy(zz, step, direction, first=0, count=PART):
        ref = blocks(zz, y, first, count)
        return remote(ref, ref, pz_sem, (direction, step), (above, below)[direction])

    def rz_copy(step, j, direction):
        zz = down(z, NZ, step) if direction == 0 else up(z, NZ, step)
        ref = blocks(zz, down(y, NY, j), PART, SHARD - PART)
        return remote(ref, ref, rz_sem, (direction, j, step), (above, below)[direction])

    def py_copy(zz, yy, direction):
        ref = blocks(zz, yy, 0, PART)
        return remote(ref, ref, py_sem, (direction, zz), (front, back)[direction])

    def pf_copy(zz, yy, direction, first):
        ref = blocks(zz, yy, *((0, HALF) if direction == first else (HALF, PART - HALF)))
        return remote(ref, ref, pf_sem, (direction, zz), (front, back)[direction])

    far = NZ // 2
    lower = [down(z, NZ, step) for step in range(far + 1)]
    upper = [up(z, NZ, step) for step in range(far + 1)]

    def p_copies(step):
        if step < far - 1:
            return [pz_copy(lower[step], step, 0), pz_copy(upper[step], step, 1)]
        return [pz_copy(lower[step], step, 0, 0, HALF), pz_copy(upper[step], step, 1, HALF, PART - HALF)]

    def r_copies(step, j):
        return [rz_copy(step, j, direction) for direction in range(2) if step < far - 1 or j // 2 == direction]

    def places_at(step):
        return [(lower[step], 0)] if step in (0, far) else [(lower[step], 0), (upper[step], 1)]

    def spread(step):
        for zz, _ in places_at(step):
            for direction in range(2):
                py_copy(zz, y, direction).start()

    def p_sent(step):
        for copy in p_copies(step):
            copy.wait_send()

    def r_sent(q):
        for copy in r_copies(q // NY, q % NY):
            copy.wait_send()

    def y_sent(step):
        for zz, first in places_at(step):
            for direction in range(2):
                pf_copy(zz, y, direction, first).wait_send()

    def p_step(step):
        sends = p_copies(step) if step < far else [None, None]
        for arrival, send in zip(p_copies(step - 1), sends):
            arrival.wait_recv()
            if send is not None:
                send.start()
        spread(step)
        if step >= 2:
            p_sent(step - 2)

    def r_step(q):
        step, j = q // NY, q % NY
        if step == 0 and j > 0:
            ry_copy(j).wait_recv()
        if step > 0:
            for copy in r_copies(step - 1, j):
                copy.wait_recv()
        if step < far:
            for copy in r_copies(step, j):
                copy.start()
        if q >= 8:
            r_sent(q - 8)

    def y_step(step):
        for zz, first in places_at(step):
            for direction, yy in ((0, down(y, NY)), (1, up(y, NY))):
                py_copy(zz, yy, direction).wait_recv()
                pf_copy(zz, yy, direction, first).start()
        for zz, _ in places_at(step):
            for direction in range(2):
                py_copy(zz, y, direction).wait_send()
        if step >= 2:
            y_sent(step - 2)

    def t_step(part):
        if part == 0:
            t_low_right.wait_recv()
            t_pass_right.start()
            t_high_left.wait_recv()
            t_pass_left.start()
        elif part == 1:
            t_high_right.wait_recv()
            t_sibling[0].start()
            t_low_left.wait_recv()
            t_sibling[1].start()
            for i in range(GROUP - 1):
                s_copy(i).wait_recv()
            places.start()
        else:
            t_from_right.wait_recv()
            t_from_left.wait_recv()
            t_sibling[2].start()
            local[0].wait()
            t_own_sibling.wait_recv()
            for copy in t_sibling[:2]:
                copy.wait_recv()
            places.wait()

    for j in range(1, NY):
        ry_copy(j).start()
    for copy in p_copies(0):
        copy.start()
    spread(0)
    steps = {"P": p_step, "R": r_step, "Y": y_step, "T": t_step}
    for entry in " ".join(ORDER).split():
        steps[entry[0]](int(entry[1:]))
    for j in range(NY):
        for copy in r_copies(far - 1, j):
            copy.wait_recv()

    for step in range(far + 1):
        for zz, first in places_at(step):
            for direction in range(2):
                pf_copy(zz, up(y, NY, 2), direction, first).wait_recv()

    t_sibling[2].wait_recv()

    def aggregate(e):
        total = jnp.zeros((COLS, BLK), jnp.float32)
        for first in range(0, SLOTS, UNROLL):
            slots = range(first, first + UNROLL)
            picked = jnp.concatenate([hb[ss[e, 0, t]] for t in slots], axis=1)
            values = jnp.concatenate([tbuf[e, t] for t in slots], axis=1)
            total += lax.dot_general(
                picked, values, (((1,), (1,)), ((), ())), preferred_element_type=jnp.float32
            )
        return jnp.maximum(total + bt[pl.ds(pl.multiple_of(c * COLS, COLS), COLS), :], 0.0).astype(jnp.bfloat16)

    def o_copy(i):
        _, device = group_peer(i)
        return remote(obuf.at[i], rbuf.at[me], o_sem, (i,), device)

    @pl.loop(0, GROUP - 1)
    def _(i):
        e, _ = group_peer(i)
        obuf[i] = aggregate(e)
        o_copy(i).start()

    rbuf[me] = aggregate(me)

    for copy in x_plane:
        copy.wait_send()

    def w_over(i):
        w_copy(i).wait_send()
        hand_on(i).wait_send()

    w_shares(w_over)

    for i in range(GROUP - 1):
        s_copy(i).wait_send()
    for copy in (t_low_right, t_high_left, t_high_right, t_low_left, t_own_sibling, t_pass_right, t_pass_left, h_copy):
        copy.wait_send()
    for copy in t_sibling:
        copy.wait_send()
    for j in range(1, NY):
        ry_copy(j).wait_send()

    p_sent(far - 1)
    for q in range(NY * far - 8, NY * far):
        r_sent(q)
    for step in (far - 1, far):
        y_sent(step)

    @pl.loop(0, GROUP - 1)
    def _(i):
        o_copy(i).wait_recv()

    out[...] = rbuf[...].reshape(GROUP * COLS, BLK).T

    @pl.loop(0, GROUP - 1)
    def _(i):
        o_copy(i).wait_send()


def shards(features, weight, bias, tile_src, tile_count, tile_vals):
    rows, depth = features.shape
    vmem = pl.BlockSpec(memory_space=pltpu.VMEM)
    hbm = pl.BlockSpec(memory_space=pltpu.HBM)
    smem = pl.BlockSpec(memory_space=pltpu.SMEM)
    dma = pltpu.SemaphoreType.DMA
    bf16 = jnp.bfloat16
    return pl.pallas_call(
        kernel,
        out_shape=jax.ShapeDtypeStruct((BLK, GROUP * COLS), bf16),
        in_specs=[hbm, hbm, hbm, hbm, smem, hbm],
        out_specs=vmem,
        scratch_shapes=[
            pltpu.VMEM((NX * NY, depth, rows // NY), bf16),
            pltpu.VMEM((NX * NY, depth, 128), bf16),
            pltpu.VMEM((BLOCKS + 1, COLS, BLK), bf16),
            pltpu.VMEM((4, COLS, BLK), bf16),
            pltpu.VMEM((GROUP, SLOTS, BLK, BLK), bf16),
            pltpu.VMEM((GROUP, 8, 128), jnp.int32),
            pltpu.SMEM((GROUP, 8, 128), jnp.int32),
            pltpu.VMEM((128, 128), jnp.float32),
            pltpu.VMEM((GROUP, COLS, BLK), bf16),
            pltpu.VMEM((GROUP, COLS, BLK), bf16),
            pltpu.VMEM((NX, 128), jnp.float32),
            pltpu.VMEM((1, SLOTS), jnp.int32),
            dma((2, NX * NY - 1)),
            dma((2, NX * NY - 1)),
            dma((2, NX * NY - 1)),
            dma((2, GROUP - 1)),
            dma((1,)),
            dma((2, 10)),
            dma((5,)),
            dma((2, 1)),
            dma((2, NY - 1)),
            dma((2, 2, NZ // 2)),
            dma((2, 2, NY, NZ // 2)),
            dma((2, 2, NZ)),
            dma((2, 2, NZ)),
            dma((2, GROUP - 1)),
        ],
        compiler_params=pltpu.CompilerParams(
            collective_id=0, has_side_effects=True, vmem_limit_bytes=56 * 2**20
        ),
    )(features.T, weight, bias.reshape(NX, 128), tile_src, tile_count, tile_vals)


def solution(mesh):
    placed = (
        P("node", "feat"),
        P("feat", None),
        P(),
        P(("node", "feat"), None),
        P(("node", "feat")),
        P(("node", "feat"), None, None, None),
    )
    return jax.shard_map(
        shards, mesh=mesh, in_specs=placed, out_specs=P(("node", "feat"), None), check_vma=False
    )
```

```python
import jax
import jax.numpy as jnp
from jax import lax
from jax.experimental import pallas as pl
from jax.experimental.pallas import tpu as pltpu
from jax.sharding import PartitionSpec as P

MESH = pl.DeviceIdType.MESH
NX, NY, NZ = 4, 4, 16
BLK = 128
COLS = 64
GROUP = 2 * NX
PART = 5
SHARD = 8
HALF = 3
BLOCKS = NZ * NY * SHARD
SLOTS = 32
UNROLL = 32
ROWS = 512
DEPTH = 768
ORDER = (
    "R1 R2 R3 P1", "R4 Y0 R5 R6", "P2 R7 Y1 R8", "R9 P3 R10 Y2",
    "R11 R12 P4 R13", "R14 Y3 R15 P5", "T0 R16 R17 Y4", "R18 P6 R19 R20",
    "Y5 R21 P7 T1", "R22 R23 R24 P8", "R25 R26 Y6 R27", "T2 R28 R30 Y7",
    "R29 R31 Y8",
)
PLANE = (
    (2, 2), (2, 1), (1, 2), (2, 3), (3, 2), (1, 1), (3, 3), (1, 3), (3, 1), (2, 0), (0, 2), (1, 0), (3, 0), (0, 1), (0, 3),
)


def kernel(
    ft, w, bias, src, cnt, tiles, out,
    xbuf, wbuf, hb, stage, tbuf, sv, ss, bt, obuf, rbuf,
    bv, iv, wt, x_sem, w_sem, v_sem, s_sem, ss_sem, t_sem, local_sem, h_sem, ry_sem, pz_sem, rz_sem, py_sem, pf_sem, o_sem,
):
    n = lax.axis_index("node")
    f = lax.axis_index("feat")
    z, c = lax.div(n, 2), lax.rem(n, 2)
    x, y = lax.div(f, NY), lax.rem(f, NY)
    me = x * 2 + c

    def at(xx, yy, zz, cc):
        return (zz * 2 + cc, xx * NY + yy)

    def up(value, size, by=1):
        return lax.rem(value + by, size)

    def down(value, size, by=1):
        return lax.rem(value + size - by, size)

    def remote(source, target, sems, index, device):
        return pltpu.make_async_remote_copy(
            src_ref=source, dst_ref=target, send_sem=sems.at[(0,) + index], recv_sem=sems.at[(1,) + index],
            device_id=device, device_id_type=MESH,
        )

    sibling = at(x, y, z, 1 - c)
    right, left = at(up(x, NX), y, z, c), at(down(x, NX), y, z, c)
    front, back = at(x, up(y, NY), z, c), at(x, down(y, NY), z, c)
    above, below = at(x, y, up(z, NZ), c), at(x, y, down(z, NZ), c)

    def group_peer(i):
        dx, dc = lax.rem(1 + lax.div(i, 2), NX), 1 - lax.rem(i, 2)
        xx, cc = up(x, NX, dx), lax.rem(c + dc, 2)
        return xx * 2 + cc, at(xx, y, z, cc)

    def group_source(i):
        dx, dc = lax.rem(1 + lax.div(i, 2), NX), 1 - lax.rem(i, 2)
        return down(x, NX, dx) * 2 + lax.rem(c + dc, 2)

    barrier = pltpu.get_barrier_semaphore()

    @pl.loop(1, NX * NY)
    def _(i):
        pl.semaphore_signal(barrier, inc=1, device_id=(n, lax.rem(f + i, NX * NY)), device_id_type=MESH)

    for i in range(1, NX):
        pl.semaphore_signal(barrier, inc=1, device_id=at(up(x, NX, i), y, z, 1 - c), device_id_type=MESH)
    for device in (sibling, above, below):
        pl.semaphore_signal(barrier, inc=1, device_id=device, device_id_type=MESH)

    def x_rows(yy, phase):
        return pl.ds(pl.multiple_of(yy * ROWS + (1 - phase) * (ROWS // 2), ROWS // 2), ROWS // 2)

    local = [
        pltpu.make_async_copy(source, target, local_sem.at[i])
        for i, (source, target) in enumerate((
            (tiles.at[0], tbuf.at[me]),
            (bias, bv),
            (src, iv),
            (ft.at[:, x_rows(y, 0)], xbuf.at[0, len(PLANE)]),
            (ft.at[:, x_rows(y, 1)], xbuf.at[1, len(PLANE)]),
            (w.at[:, pl.ds(pl.multiple_of(x * 128, 128), 128)], wbuf.at[len(PLANE)]),
        ))
    ]
    for copy in local:
        copy.start()

    pl.semaphore_wait(barrier, NX * NY - 1 + NX - 1 + 3)

    def plane_peer(i):
        dx, dy = PLANE[i]
        return up(x, NX, dx), up(y, NY, dy)

    def x_copy(i, phase):
        xx, yy = plane_peer(i)
        return remote(
            ft.at[:, x_rows(yy, phase)], xbuf.at[phase, i], x_sem, (phase, i), at(xx, yy, z, c)
        )

    def w_copy(i):
        xx, yy = plane_peer(i)
        columns = pl.ds(pl.multiple_of(xx * 128, 128), 128)
        return remote(w.at[:, columns], wbuf.at[i], w_sem, (i,), at(xx, yy, z, c))

    def w_shares(method):
        for core in range(2):

            @pl.when(c == core)
            def _():
                for i in range(core, len(PLANE), 2):
                    method(i)

    w_shares(lambda i: w_copy(i).start())
    x_plane = [[x_copy(i, phase) for i in range(len(PLANE))] for phase in range(2)]
    for copy in x_plane[0] + x_plane[1]:
        copy.start()

    hb[BLOCKS] = jnp.zeros((COLS, BLK), jnp.bfloat16)
    local[1].wait()
    bt[...] = jnp.broadcast_to(bv[pl.ds(x, 1), :], (128, 128)).T
    local[2].wait()
    s = iv[...]
    zz, rest = lax.shift_right_logical(s, 5), s & 31
    cc, ff = lax.shift_right_logical(rest, 4), rest & 15
    place = (zz * NY + lax.shift_right_logical(ff, 2)) * SHARD + (ff & 2) * 2 + cc * 2 + (ff & 1)
    alive = lax.broadcasted_iota(jnp.int32, s.shape, 1) < cnt[0]
    sv[me] = jnp.zeros((8, 128), jnp.int32)
    sv[me, 0:1, 0:SLOTS] = jnp.where(alive, place, BLOCKS)

    def s_copy(i):
        _, device = group_peer(i)
        return remote(sv.at[me], sv.at[me], s_sem, (i,), device)

    for i in range(GROUP - 1):
        s_copy(i).start()
    local[5].wait()
    def hand_on(i):
        return remote(wbuf.at[i], wbuf.at[i], v_sem, (i,), sibling)

    def pass_weights(i):
        w_copy(i).wait_recv()
        hand_on(i).start()

    w_shares(pass_weights)
    for core in range(2):

        @pl.when(c == core)
        def _():
            for i in range(1 - core, len(PLANE), 2):
                hand_on(i).wait_recv()

    wt[...] = wbuf[...].reshape(DEPTH, 128).T

    def transform(core, phase):
        columns = wt[pl.ds(pl.multiple_of(core * COLS, COLS), COLS), :]
        hidden = jnp.dot(columns, xbuf[phase].reshape(DEPTH, ROWS // 2), preferred_element_type=jnp.float32)
        return hidden.astype(jnp.bfloat16)

    def place_of(zz, yy):
        return (zz * NY + yy) * SHARD

    def h_copy(phase):
        base = place_of(z, y) + 4 * (1 - phase) + 2 * c
        return remote(stage.at[pl.ds(2 * phase, 2)], hb.at[pl.ds(base, 2)], h_sem, (phase,), sibling)

    def make_hidden(phase):
        other = transform(1 - c, phase)
        for k in range(2):
            stage[2 * phase + k] = other[:, k * BLK : (k + 1) * BLK]
        h_copy(phase).start()
        mine = transform(c, phase)
        for k in range(2):
            hb[place_of(z, y) + 4 * (1 - phase) + 2 * c + k] = mine[:, k * BLK : (k + 1) * BLK]

    local[3].wait()
    for copy in x_plane[0]:
        copy.wait_recv()
    make_hidden(0)
    h_copy(0).wait_recv()

    def blocks(zz, yy, first, count):
        return hb.at[pl.ds(place_of(zz, yy) + first, count)]

    def ry_copy(j):
        ref = blocks(z, y, PART, SHARD - PART)
        return remote(ref, ref, ry_sem, (j - 1,), at(x, up(y, NY, j), z, c))

    def pz_copy(zz, step, direction, first=0, count=PART):
        ref = blocks(zz, y, first, count)
        return remote(ref, ref, pz_sem, (direction, step), (above, below)[direction])

    def rz_copy(step, j, direction):
        zz = down(z, NZ, step) if direction == 0 else up(z, NZ, step)
        ref = blocks(zz, down(y, NY, j), PART, SHARD - PART)
        return remote(ref, ref, rz_sem, (direction, j, step), (above, below)[direction])

    def py_copy(zz, yy, direction):
        ref = blocks(zz, yy, 0, PART)
        return remote(ref, ref, py_sem, (direction, zz), (front, back)[direction])

    def pf_copy(zz, yy, direction, first):
        ref = blocks(zz, yy, *((0, HALF) if direction == first else (HALF, PART - HALF)))
        return remote(ref, ref, pf_sem, (direction, zz), (front, back)[direction])

    far = NZ // 2
    lower = [down(z, NZ, step) for step in range(far + 1)]
    upper = [up(z, NZ, step) for step in range(far + 1)]

    def p_copies(step):
        if step < far - 1:
            return [pz_copy(lower[step], step, 0), pz_copy(upper[step], step, 1)]
        return [pz_copy(lower[step], step, 0, 0, HALF), pz_copy(upper[step], step, 1, HALF, PART - HALF)]

    def r_copies(step, j):
        return [rz_copy(step, j, direction) for direction in range(2) if step < far - 1 or j // 2 == direction]

    def places_at(step):
        return [(lower[step], 0)] if step in (0, far) else [(lower[step], 0), (upper[step], 1)]

    def spread(step):
        for zz, _ in places_at(step):
            for direction in range(2):
                py_copy(zz, y, direction).start()

    def p_sent(step):
        for copy in p_copies(step):
            copy.wait_send()

    def r_sent(q):
        for copy in r_copies(q // NY, q % NY):
            copy.wait_send()

    def y_sent(step):
        for zz, first in places_at(step):
            for direction in range(2):
                pf_copy(zz, y, direction, first).wait_send()

    def p_step(step):
        sends = p_copies(step) if step < far else [None, None]
        for arrival, send in zip(p_copies(step - 1), sends):
            arrival.wait_recv()
            if send is not None:
                send.start()
        spread(step)
        if step >= 2:
            p_sent(step - 2)

    def r_step(q):
        step, j = q // NY, q % NY
        if step == 0 and j > 0:
            ry_copy(j).wait_recv()
        if step > 0:
            for copy in r_copies(step - 1, j):
                copy.wait_recv()
        if step < far:
            for copy in r_copies(step, j):
                copy.start()
        if q >= 8:
            r_sent(q - 8)

    def y_step(step):
        for zz, first in places_at(step):
            for direction, yy in ((0, down(y, NY)), (1, up(y, NY))):
                py_copy(zz, yy, direction).wait_recv()
                pf_copy(zz, yy, direction, first).start()
        for zz, _ in places_at(step):
            for direction in range(2):
                py_copy(zz, y, direction).wait_send()
        if step >= 2:
            y_sent(step - 2)

    def t_step(part):
        if part == 0:
            t_low_right.wait_recv()
            t_pass_right.start()
            t_high_left.wait_recv()
            t_pass_left.start()
        elif part == 1:
            t_high_right.wait_recv()
            t_sibling[0].start()
            t_low_left.wait_recv()
            t_sibling[1].start()
            for i in range(GROUP - 1):
                s_copy(i).wait_recv()
            places.start()
        else:
            t_from_right.wait_recv()
            t_from_left.wait_recv()
            t_sibling[2].start()
            local[0].wait()
            t_own_sibling.wait_recv()
            for copy in t_sibling[:2]:
                copy.wait_recv()
            places.wait()

    for j in range(1, NY):
        ry_copy(j).start()
    r_step(0)

    own = tiles.at[0]
    low, high = pl.ds(0, SLOTS // 2), pl.ds(SLOTS // 2, SLOTS // 2)
    t_low_right = remote(own.at[low], tbuf.at[me, low], t_sem, (0,), right)
    t_high_left = remote(own.at[high], tbuf.at[me, high], t_sem, (1,), left)
    t_high_right = remote(own.at[high], tbuf.at[me, high], t_sem, (2,), right)
    t_low_left = remote(own.at[low], tbuf.at[me, low], t_sem, (3,), left)
    t_own_sibling = remote(own, tbuf.at[me], t_sem, (4,), sibling)
    from_left, from_right, from_far = (down(x, NX) * 2 + c, up(x, NX) * 2 + c, up(x, NX, 2) * 2 + c)
    t_pass_right = remote(tbuf.at[from_left, low], tbuf.at[from_left, low], t_sem, (5,), right)
    t_pass_left = remote(tbuf.at[from_right, high], tbuf.at[from_right, high], t_sem, (6,), left)
    t_sibling = [
        remote(tbuf.at[e], tbuf.at[e], t_sem, (7 + j,), sibling)
        for j, e in enumerate((from_left, from_right, from_far))
    ]

    t_from_right = remote(tbuf.at[from_far, low], tbuf.at[from_far, low], t_sem, (5,), right)
    t_from_left = remote(tbuf.at[from_far, high], tbuf.at[from_far, high], t_sem, (6,), left)
    places = pltpu.make_async_copy(sv, ss, ss_sem.at[0])

    local[4].wait()
    for copy in x_plane[1]:
        copy.wait_recv()
    make_hidden(1)
    for copy in (t_low_right, t_high_left, t_high_right, t_low_left, t_own_sibling):
        copy.start()
    h_copy(1).wait_recv()
    for copy in p_copies(0):
        copy.start()
    spread(0)
    steps = {"P": p_step, "R": r_step, "Y": y_step, "T": t_step}
    for entry in " ".join(ORDER).split():
        steps[entry[0]](int(entry[1:]))
    for j in range(NY):
        for copy in r_copies(far - 1, j):
            copy.wait_recv()

    for step in range(far + 1):
        for zz, first in places_at(step):
            for direction in range(2):
                pf_copy(zz, up(y, NY, 2), direction, first).wait_recv()

    t_sibling[2].wait_recv()

    def aggregate(e):
        total = jnp.zeros((COLS, BLK), jnp.float32)
        for first in range(0, SLOTS, UNROLL):
            slots = range(first, first + UNROLL)
            picked = jnp.concatenate([hb[ss[e, 0, t]] for t in slots], axis=1)
            values = jnp.concatenate([tbuf[e, t] for t in slots], axis=1)
            total += lax.dot_general(
                picked, values, (((1,), (1,)), ((), ())), preferred_element_type=jnp.float32
            )
        return jnp.maximum(total + bt[pl.ds(pl.multiple_of(c * COLS, COLS), COLS), :], 0.0).astype(jnp.bfloat16)

    def o_copy(i):
        _, device = group_peer(i)
        return remote(obuf.at[i], rbuf.at[me], o_sem, (i,), device)

    @pl.loop(0, GROUP - 1)
    def _(i):
        e, _ = group_peer(i)
        obuf[i] = aggregate(e)
        o_copy(i).start()

    rbuf[me] = aggregate(me)

    for copy in x_plane[0] + x_plane[1]:
        copy.wait_send()

    def w_over(i):
        w_copy(i).wait_send()
        hand_on(i).wait_send()

    w_shares(w_over)

    for i in range(GROUP - 1):
        s_copy(i).wait_send()
    for copy in (t_low_right, t_high_left, t_high_right, t_low_left, t_own_sibling, t_pass_right, t_pass_left, h_copy(0), h_copy(1)):
        copy.wait_send()
    for copy in t_sibling:
        copy.wait_send()
    for j in range(1, NY):
        ry_copy(j).wait_send()

    p_sent(far - 1)
    for q in range(NY * far - 8, NY * far):
        r_sent(q)
    for step in (far - 1, far):
        y_sent(step)

    @pl.loop(0, GROUP - 1)
    def _(i):
        o_copy(i).wait_recv()

    out[...] = rbuf[...].reshape(GROUP * COLS, BLK).T

    @pl.loop(0, GROUP - 1)
    def _(i):
        o_copy(i).wait_send()


def shards(features, weight, bias, tile_src, tile_count, tile_vals):
    rows, depth = features.shape
    vmem = pl.BlockSpec(memory_space=pltpu.VMEM)
    hbm = pl.BlockSpec(memory_space=pltpu.HBM)
    smem = pl.BlockSpec(memory_space=pltpu.SMEM)
    dma = pltpu.SemaphoreType.DMA
    bf16 = jnp.bfloat16
    return pl.pallas_call(
        kernel,
        out_shape=jax.ShapeDtypeStruct((BLK, GROUP * COLS), bf16),
        in_specs=[hbm, hbm, hbm, hbm, smem, hbm],
        out_specs=vmem,
        scratch_shapes=[
            pltpu.VMEM((2, NX * NY, depth, ROWS // 2), bf16),
            pltpu.VMEM((NX * NY, depth, 128), bf16),
            pltpu.VMEM((BLOCKS + 1, COLS, BLK), bf16),
            pltpu.VMEM((4, COLS, BLK), bf16),
            pltpu.VMEM((GROUP, SLOTS, BLK, BLK), bf16),
            pltpu.VMEM((GROUP, 8, 128), jnp.int32),
            pltpu.SMEM((GROUP, 8, 128), jnp.int32),
            pltpu.VMEM((128, 128), jnp.float32),
            pltpu.VMEM((GROUP, COLS, BLK), bf16),
            pltpu.VMEM((GROUP, COLS, BLK), bf16),
            pltpu.VMEM((NX, 128), jnp.float32),
            pltpu.VMEM((1, SLOTS), jnp.int32),
            pltpu.VMEM((128, DEPTH), bf16),
            dma((2, 2, NX * NY - 1)),
            dma((2, NX * NY - 1)),
            dma((2, NX * NY - 1)),
            dma((2, GROUP - 1)),
            dma((1,)),
            dma((2, 10)),
            dma((6,)),
            dma((2, 2)),
            dma((2, NY - 1)),
            dma((2, 2, NZ // 2)),
            dma((2, 2, NY, NZ // 2)),
            dma((2, 2, NZ)),
            dma((2, 2, NZ)),
            dma((2, GROUP - 1)),
        ],
        compiler_params=pltpu.CompilerParams(
            collective_id=0, has_side_effects=True, vmem_limit_bytes=56 * 2**20
        ),
    )(features.T, weight, bias.reshape(NX, 128), tile_src, tile_count, tile_vals)


def solution(mesh):
    placed = (
        P("node", "feat"),
        P("feat", None),
        P(),
        P(("node", "feat"), None),
        P(("node", "feat")),
        P(("node", "feat"), None, None, None),
    )
    return jax.shard_map(
        shards, mesh=mesh, in_specs=placed, out_specs=P(("node", "feat"), None), check_vma=False
    )
```

```python
import jax
import jax.numpy as jnp
from jax import lax
from jax.experimental import pallas as pl
from jax.experimental.pallas import tpu as pltpu
from jax.sharding import PartitionSpec as P

MESH = pl.DeviceIdType.MESH
NX, NY, NZ = 4, 4, 16
BLK = 128
COLS = 64
GROUP = 2 * NX
PART = 5
SHARD = 8
HALF = 3
BLOCKS = NZ * NY * SHARD
SLOTS = 32
UNROLL = 32
ROWS = 512
DEPTH = 768
DIRECT, RELAYED = 11, 4
ORDER = (
    "R0 R1 P1 R2", "Y0 R3 R4 P2", "R5 Y1 R6 R7", "P3 R8 Y2 R9",
    "R10 P4 R11 R12", "Y3 R13 P5 T0", "R14 R15 Y4 R16", "P6 R17 R18 Y5",
    "R19 P7 T1 R20", "R21 R22 P8 R23", "R24 Y6 R25 R26", "T2 Y7 R27 Y8",
    "R28 R30 R29 R31",
)
PLANE = (
    (1, 0), (3, 1), (1, 2), (3, 3), (1, 1), (3, 0), (1, 3), (3, 2), (0, 1), (0, 3), (0, 2), (2, 0), (2, 1), (2, 2), (2, 3),
)


def kernel(
    ft, w, bias, src, cnt, tiles, out,
    xbuf, wbuf, hb, stage, tbuf, sv, ss, bt, obuf, rbuf,
    bv, iv, wt, ht, r_sem, x_sem, w_sem, v_sem, s_sem, ss_sem, t_sem, local_sem, h_sem, ry_sem, pz_sem, rz_sem, py_sem, pf_sem, o_sem,
):
    n = lax.axis_index("node")
    f = lax.axis_index("feat")
    z, c = lax.div(n, 2), lax.rem(n, 2)
    x, y = lax.div(f, NY), lax.rem(f, NY)
    me = x * 2 + c

    def at(xx, yy, zz, cc):
        return (zz * 2 + cc, xx * NY + yy)

    def up(value, size, by=1):
        return lax.rem(value + by, size)

    def down(value, size, by=1):
        return lax.rem(value + size - by, size)

    def remote(source, target, sems, index, device):
        return pltpu.make_async_remote_copy(
            src_ref=source, dst_ref=target, send_sem=sems.at[(0,) + index], recv_sem=sems.at[(1,) + index],
            device_id=device, device_id_type=MESH,
        )

    sibling = at(x, y, z, 1 - c)
    right, left = at(up(x, NX), y, z, c), at(down(x, NX), y, z, c)
    front, back = at(x, up(y, NY), z, c), at(x, down(y, NY), z, c)
    above, below = at(x, y, up(z, NZ), c), at(x, y, down(z, NZ), c)

    def group_peer(i):
        dx, dc = lax.rem(1 + lax.div(i, 2), NX), 1 - lax.rem(i, 2)
        xx, cc = up(x, NX, dx), lax.rem(c + dc, 2)
        return xx * 2 + cc, at(xx, y, z, cc)

    def group_source(i):
        dx, dc = lax.rem(1 + lax.div(i, 2), NX), 1 - lax.rem(i, 2)
        return down(x, NX, dx) * 2 + lax.rem(c + dc, 2)

    barrier = pltpu.get_barrier_semaphore()

    @pl.loop(1, NX * NY)
    def _(i):
        pl.semaphore_signal(barrier, inc=1, device_id=(n, lax.rem(f + i, NX * NY)), device_id_type=MESH)

    for i in range(1, NX):
        pl.semaphore_signal(barrier, inc=1, device_id=at(up(x, NX, i), y, z, 1 - c), device_id_type=MESH)
    for device in (sibling, above, below):
        pl.semaphore_signal(barrier, inc=1, device_id=device, device_id_type=MESH)

    local = [
        pltpu.make_async_copy(source, target, local_sem.at[i])
        for i, (source, target) in enumerate((
            (tiles.at[0], tbuf.at[me]),
            (bias, bv),
            (src, iv),
            (ft.at[:, pl.ds(pl.multiple_of(y * ROWS, ROWS), ROWS)], xbuf.at[len(PLANE)]),
            (w.at[:, pl.ds(pl.multiple_of(x * 128, 128), 128)], wbuf.at[len(PLANE)]),
        ))
    ]
    for copy in local:
        copy.start()

    pl.semaphore_wait(barrier, NX * NY - 1 + NX - 1 + 3)

    def plane_peer(i):
        dx, dy = PLANE[i]
        return up(x, NX, dx), up(y, NY, dy)

    def x_copy(i):
        xx, yy = plane_peer(i)
        rows = pl.ds(pl.multiple_of(yy * ROWS, ROWS), ROWS)
        return remote(ft.at[:, rows], xbuf.at[i], x_sem, (i,), at(xx, yy, z, c))

    def w_copy(i):
        xx, yy = plane_peer(i)
        columns = pl.ds(pl.multiple_of(xx * 128, 128), 128)
        return remote(w.at[:, columns], wbuf.at[i], w_sem, (i,), at(xx, yy, z, c))

    def w_shares(method):
        for core in range(2):

            @pl.when(c == core)
            def _():
                for i in range(core, len(PLANE), 2):
                    method(i)

    x_plane = [x_copy(i) for i in range(DIRECT)]
    for copy in x_plane[:RELAYED]:
        copy.start()
    w_shares(lambda i: w_copy(i).start())
    for copy in x_plane[RELAYED:]:
        copy.start()

    def relay(i):
        return remote(xbuf.at[i], xbuf.at[DIRECT + i], r_sem, (i,), (right, left)[i % 2])

    hb[BLOCKS] = jnp.zeros((COLS, BLK), jnp.bfloat16)
    local[1].wait()
    bt[...] = jnp.broadcast_to(bv[pl.ds(x, 1), :], (128, 128)).T
    local[2].wait()
    s = iv[...]
    zz, rest = lax.shift_right_logical(s, 5), s & 31
    cc, ff = lax.shift_right_logical(rest, 4), rest & 15
    place = (zz * NY + lax.shift_right_logical(ff, 2)) * SHARD + cc * 4 + (ff & 3)
    alive = lax.broadcasted_iota(jnp.int32, s.shape, 1) < cnt[0]
    sv[me] = jnp.zeros((8, 128), jnp.int32)
    sv[me, 0:1, 0:SLOTS] = jnp.where(alive, place, BLOCKS)

    def s_copy(i):
        _, device = group_peer(i)
        return remote(sv.at[me], sv.at[me], s_sem, (i,), device)

    for i in range(GROUP - 1):
        s_copy(i).start()
    local[4].wait()
    def hand_on(i):
        return remote(wbuf.at[i], wbuf.at[i], v_sem, (i,), sibling)

    def pass_weights(i):
        w_copy(i).wait_recv()
        hand_on(i).start()

    w_shares(pass_weights)
    relays = [relay(i) for i in range(RELAYED)]
    for arrival, copy in zip(x_plane, relays):
        arrival.wait_recv()
        copy.start()
    for core in range(2):

        @pl.when(c == core)
        def _():
            for i in range(1 - core, len(PLANE), 2):
                hand_on(i).wait_recv()

    wt[...] = wbuf[...].reshape(DEPTH, 128).T
    half = DEPTH // 2

    def transform(core, part):
        columns = wt[pl.ds(pl.multiple_of(core * COLS, COLS), COLS), part * half : (part + 1) * half]
        rows = xbuf[part * 8 : (part + 1) * 8].reshape(half, ROWS)
        return jnp.dot(columns, rows, preferred_element_type=jnp.float32)

    for copy in x_plane[RELAYED:8]:
        copy.wait_recv()
    for core in range(2):
        ht[core] = transform(core, 0)
    local[3].wait()
    for copy in x_plane[8:] + relays:
        copy.wait_recv()

    own = tiles.at[0]
    low, high = pl.ds(0, SLOTS // 2), pl.ds(SLOTS // 2, SLOTS // 2)
    t_low_right = remote(own.at[low], tbuf.at[me, low], t_sem, (0,), right)
    t_high_left = remote(own.at[high], tbuf.at[me, high], t_sem, (1,), left)
    t_high_right = remote(own.at[high], tbuf.at[me, high], t_sem, (2,), right)
    t_low_left = remote(own.at[low], tbuf.at[me, low], t_sem, (3,), left)
    t_own_sibling = remote(own, tbuf.at[me], t_sem, (4,), sibling)
    for copy in (t_low_right, t_high_left, t_high_right, t_low_left):
        copy.start()
    from_left, from_right, from_far = (down(x, NX) * 2 + c, up(x, NX) * 2 + c, up(x, NX, 2) * 2 + c)
    t_pass_right = remote(tbuf.at[from_left, low], tbuf.at[from_left, low], t_sem, (5,), right)
    t_pass_left = remote(tbuf.at[from_right, high], tbuf.at[from_right, high], t_sem, (6,), left)
    t_sibling = [
        remote(tbuf.at[e], tbuf.at[e], t_sem, (7 + j,), sibling)
        for j, e in enumerate((from_left, from_right, from_far))
    ]

    t_from_right = remote(tbuf.at[from_far, low], tbuf.at[from_far, low], t_sem, (5,), right)
    t_from_left = remote(tbuf.at[from_far, high], tbuf.at[from_far, high], t_sem, (6,), left)
    places = pltpu.make_async_copy(sv, ss, ss_sem.at[0])

    place_of = lambda zz, yy: (zz * NY + yy) * SHARD
    base = place_of(z, y) + c * 4
    other = (ht[1 - c] + transform(1 - c, 1)).astype(jnp.bfloat16)
    for k in range(4):
        stage[k] = other[:, k * BLK : (k + 1) * BLK]
    h_copy = remote(stage, hb.at[pl.ds(base, 4)], h_sem, (0,), sibling)
    h_copy.start()
    t_own_sibling.start()
    mine = (ht[c] + transform(c, 1)).astype(jnp.bfloat16)
    for k in range(4):
        hb[base + k] = mine[:, k * BLK : (k + 1) * BLK]
    h_copy.wait_recv()

    def blocks(zz, yy, first, count):
        return hb.at[pl.ds(place_of(zz, yy) + first, count)]

    def ry_copy(j):
        ref = blocks(z, y, PART, SHARD - PART)
        return remote(ref, ref, ry_sem, (j - 1,), at(x, up(y, NY, j), z, c))

    def pz_copy(zz, step, direction, first=0, count=PART):
        ref = blocks(zz, y, first, count)
        return remote(ref, ref, pz_sem, (direction, step), (above, below)[direction])

    def rz_copy(step, j, direction):
        zz = down(z, NZ, step) if direction == 0 else up(z, NZ, step)
        ref = blocks(zz, down(y, NY, j), PART, SHARD - PART)
        return remote(ref, ref, rz_sem, (direction, j, step), (above, below)[direction])

    def py_copy(zz, yy, direction):
        ref = blocks(zz, yy, 0, PART)
        return remote(ref, ref, py_sem, (direction, zz), (front, back)[direction])

    def pf_copy(zz, yy, direction, first):
        ref = blocks(zz, yy, *((0, HALF) if direction == first else (HALF, PART - HALF)))
        return remote(ref, ref, pf_sem, (direction, zz), (front, back)[direction])

    far = NZ // 2
    lower = [down(z, NZ, step) for step in range(far + 1)]
    upper = [up(z, NZ, step) for step in range(far + 1)]

    def p_copies(step):
        if step < far - 1:
            return [pz_copy(lower[step], step, 0), pz_copy(upper[step], step, 1)]
        return [pz_copy(lower[step], step, 0, 0, HALF), pz_copy(upper[step], step, 1, HALF, PART - HALF)]

    def r_copies(step, j):
        return [rz_copy(step, j, direction) for direction in range(2) if step < far - 1 or j // 2 == direction]

    def places_at(step):
        return [(lower[step], 0)] if step in (0, far) else [(lower[step], 0), (upper[step], 1)]

    def spread(step):
        for zz, _ in places_at(step):
            for direction in range(2):
                py_copy(zz, y, direction).start()

    def p_sent(step):
        for copy in p_copies(step):
            copy.wait_send()

    def r_sent(q):
        for copy in r_copies(q // NY, q % NY):
            copy.wait_send()

    def y_sent(step):
        for zz, first in places_at(step):
            for direction in range(2):
                pf_copy(zz, y, direction, first).wait_send()

    def p_step(step):
        sends = p_copies(step) if step < far else [None, None]
        for arrival, send in zip(p_copies(step - 1), sends):
            arrival.wait_recv()
            if send is not None:
                send.start()
        spread(step)
        if step >= 2:
            p_sent(step - 2)

    def r_step(q):
        step, j = q // NY, q % NY
        if step == 0 and j > 0:
            ry_copy(j).wait_recv()
        if step > 0:
            for copy in r_copies(step - 1, j):
                copy.wait_recv()
        if step < far:
            for copy in r_copies(step, j):
                copy.start()
        if q >= 8:
            r_sent(q - 8)

    def y_step(step):
        for zz, first in places_at(step):
            for direction, yy in ((0, down(y, NY)), (1, up(y, NY))):
                py_copy(zz, yy, direction).wait_recv()
                pf_copy(zz, yy, direction, first).start()
        for zz, _ in places_at(step):
            for direction in range(2):
                py_copy(zz, y, direction).wait_send()
        if step >= 2:
            y_sent(step - 2)

    def t_step(part):
        if part == 0:
            t_low_right.wait_recv()
            t_pass_right.start()
            t_high_left.wait_recv()
            t_pass_left.start()
        elif part == 1:
            t_high_right.wait_recv()
            t_sibling[0].start()
            t_low_left.wait_recv()
            t_sibling[1].start()
            for i in range(GROUP - 1):
                s_copy(i).wait_recv()
            places.start()
        else:
            t_from_right.wait_recv()
            t_from_left.wait_recv()
            t_sibling[2].start()
            local[0].wait()
            t_own_sibling.wait_recv()
            for copy in t_sibling[:2]:
                copy.wait_recv()
            places.wait()

    for j in range(1, NY):
        ry_copy(j).start()
    for copy in p_copies(0):
        copy.start()
    spread(0)
    steps = {"P": p_step, "R": r_step, "Y": y_step, "T": t_step}
    for entry in " ".join(ORDER).split():
        steps[entry[0]](int(entry[1:]))
    for j in range(NY):
        for copy in r_copies(far - 1, j):
            copy.wait_recv()

    for step in range(far + 1):
        for zz, first in places_at(step):
            for direction in range(2):
                pf_copy(zz, up(y, NY, 2), direction, first).wait_recv()

    t_sibling[2].wait_recv()

    def aggregate(e):
        total = jnp.zeros((COLS, BLK), jnp.float32)
        for first in range(0, SLOTS, UNROLL):
            slots = range(first, first + UNROLL)
            picked = jnp.concatenate([hb[ss[e, 0, t]] for t in slots], axis=1)
            values = jnp.concatenate([tbuf[e, t] for t in slots], axis=1)
            total += lax.dot_general(
                picked, values, (((1,), (1,)), ((), ())), preferred_element_type=jnp.float32
            )
        return jnp.maximum(total + bt[pl.ds(pl.multiple_of(c * COLS, COLS), COLS), :], 0.0).astype(jnp.bfloat16)

    def o_copy(i):
        _, device = group_peer(i)
        return remote(obuf.at[i], rbuf.at[me], o_sem, (i,), device)

    @pl.loop(0, GROUP - 1)
    def _(i):
        e, _ = group_peer(i)
        obuf[i] = aggregate(e)
        o_copy(i).start()

    rbuf[me] = aggregate(me)

    for copy in x_plane + relays:
        copy.wait_send()

    def w_over(i):
        w_copy(i).wait_send()
        hand_on(i).wait_send()

    w_shares(w_over)

    for i in range(GROUP - 1):
        s_copy(i).wait_send()
    for copy in (t_low_right, t_high_left, t_high_right, t_low_left, t_own_sibling, t_pass_right, t_pass_left, h_copy):
        copy.wait_send()
    for copy in t_sibling:
        copy.wait_send()
    for j in range(1, NY):
        ry_copy(j).wait_send()

    p_sent(far - 1)
    for q in range(NY * far - 8, NY * far):
        r_sent(q)
    for step in (far - 1, far):
        y_sent(step)

    @pl.loop(0, GROUP - 1)
    def _(i):
        o_copy(i).wait_recv()

    out[...] = rbuf[...].reshape(GROUP * COLS, BLK).T

    @pl.loop(0, GROUP - 1)
    def _(i):
        o_copy(i).wait_send()


def shards(features, weight, bias, tile_src, tile_count, tile_vals):
    rows, depth = features.shape
    vmem = pl.BlockSpec(memory_space=pltpu.VMEM)
    hbm = pl.BlockSpec(memory_space=pltpu.HBM)
    smem = pl.BlockSpec(memory_space=pltpu.SMEM)
    dma = pltpu.SemaphoreType.DMA
    bf16 = jnp.bfloat16
    return pl.pallas_call(
        kernel,
        out_shape=jax.ShapeDtypeStruct((BLK, GROUP * COLS), bf16),
        in_specs=[hbm, hbm, hbm, hbm, smem, hbm],
        out_specs=vmem,
        scratch_shapes=[
            pltpu.VMEM((NX * NY, depth, rows // NY), bf16),
            pltpu.VMEM((NX * NY, depth, 128), bf16),
            pltpu.VMEM((BLOCKS + 1, COLS, BLK), bf16),
            pltpu.VMEM((4, COLS, BLK), bf16),
            pltpu.VMEM((GROUP, SLOTS, BLK, BLK), bf16),
            pltpu.VMEM((GROUP, 8, 128), jnp.int32),
            pltpu.SMEM((GROUP, 8, 128), jnp.int32),
            pltpu.VMEM((128, 128), jnp.float32),
            pltpu.VMEM((GROUP, COLS, BLK), bf16),
            pltpu.VMEM((GROUP, COLS, BLK), bf16),
            pltpu.VMEM((NX, 128), jnp.float32),
            pltpu.VMEM((1, SLOTS), jnp.int32),
            pltpu.VMEM((128, DEPTH), bf16),
            pltpu.VMEM((2, COLS, ROWS), jnp.float32),
            dma((2, RELAYED)),
            dma((2, NX * NY - 1)),
            dma((2, NX * NY - 1)),
            dma((2, NX * NY - 1)),
            dma((2, GROUP - 1)),
            dma((1,)),
            dma((2, 10)),
            dma((5,)),
            dma((2, 1)),
            dma((2, NY - 1)),
            dma((2, 2, NZ // 2)),
            dma((2, 2, NY, NZ // 2)),
            dma((2, 2, NZ)),
            dma((2, 2, NZ)),
            dma((2, GROUP - 1)),
        ],
        compiler_params=pltpu.CompilerParams(
            collective_id=0, has_side_effects=True, vmem_limit_bytes=56 * 2**20
        ),
    )(features.T, weight, bias.reshape(NX, 128), tile_src, tile_count, tile_vals)


def solution(mesh):
    placed = (
        P("node", "feat"),
        P("feat", None),
        P(),
        P(("node", "feat"), None),
        P(("node", "feat")),
        P(("node", "feat"), None, None, None),
    )
    return jax.shard_map(
        shards, mesh=mesh, in_specs=placed, out_specs=P(("node", "feat"), None), check_vma=False
    )
```

```python
import jax
import jax.numpy as jnp
from jax import lax
from jax.experimental import pallas as pl
from jax.experimental.pallas import tpu as pltpu
from jax.sharding import PartitionSpec as P

MESH = pl.DeviceIdType.MESH
NX, NY, NZ = 4, 4, 16
BLK = 128
COLS = 64
GROUP = 2 * NX
PART = 5
SHARD = 8
HALF = 3
BLOCKS = NZ * NY * SHARD
SLOTS = 32
UNROLL = 32
ROWS = 512
DEPTH = 768
DIRECT, RELAYED = 11, 4
ORDER = (
    "R0 R1 P1 R2", "Y0 R3 R4 P2", "R5 Y1 R6 R7", "P3 R8 Y2 R9",
    "R10 P4 R11 R12", "Y3 R13 P5 T0", "R14 R15 Y4 R16", "P6 R17 R18 Y5",
    "R19 P7 T1 R20", "R21 R22 P8 R23", "R24 Y6 R25 R26", "T2 Y7 R27 Y8",
    "R28 R30 R29 R31",
)
PLANE = (
    (1, 0), (3, 1), (1, 2), (3, 3), (1, 1), (3, 0), (1, 3), (3, 2), (0, 1), (0, 3), (0, 2), (2, 0), (2, 1), (2, 2), (2, 3),
)


def kernel(
    ft, w, bias, src, cnt, tiles, out,
    xbuf, wbuf, hb, stage, tbuf, sv, ss, bt, obuf, rbuf,
    bv, iv, wt, ht, r_sem, x_sem, w_sem, v_sem, s_sem, ss_sem, t_sem, local_sem, h_sem, ry_sem, pz_sem, rz_sem, py_sem, pf_sem, o_sem,
):
    n = lax.axis_index("node")
    f = lax.axis_index("feat")
    z, c = lax.div(n, 2), lax.rem(n, 2)
    x, y = lax.div(f, NY), lax.rem(f, NY)
    me = x * 2 + c

    def at(xx, yy, zz, cc):
        return (zz * 2 + cc, xx * NY + yy)

    def up(value, size, by=1):
        return lax.rem(value + by, size)

    def down(value, size, by=1):
        return lax.rem(value + size - by, size)

    def remote(source, target, sems, index, device):
        return pltpu.make_async_remote_copy(
            src_ref=source, dst_ref=target, send_sem=sems.at[(0,) + index], recv_sem=sems.at[(1,) + index],
            device_id=device, device_id_type=MESH,
        )

    sibling = at(x, y, z, 1 - c)
    right, left = at(up(x, NX), y, z, c), at(down(x, NX), y, z, c)
    front, back = at(x, up(y, NY), z, c), at(x, down(y, NY), z, c)
    above, below = at(x, y, up(z, NZ), c), at(x, y, down(z, NZ), c)

    def group_offset(i):
        k = lax.div(i, 2)
        return lax.rem(2 + 3 * k + 3 * lax.div(k * (k - 1), 2), NX), 1 - lax.rem(i, 2)

    def group_peer(i):
        dx, dc = group_offset(i)
        xx, cc = up(x, NX, dx), lax.rem(c + dc, 2)
        return xx * 2 + cc, at(xx, y, z, cc)

    def group_source(i):
        dx, dc = group_offset(i)
        return down(x, NX, dx) * 2 + lax.rem(c + dc, 2)

    barrier = pltpu.get_barrier_semaphore()

    @pl.loop(1, NX * NY)
    def _(i):
        pl.semaphore_signal(barrier, inc=1, device_id=(n, lax.rem(f + i, NX * NY)), device_id_type=MESH)

    for i in range(1, NX):
        pl.semaphore_signal(barrier, inc=1, device_id=at(up(x, NX, i), y, z, 1 - c), device_id_type=MESH)
    for device in (sibling, above, below):
        pl.semaphore_signal(barrier, inc=1, device_id=device, device_id_type=MESH)

    local = [
        pltpu.make_async_copy(source, target, local_sem.at[i])
        for i, (source, target) in enumerate((
            (tiles.at[0], tbuf.at[me]),
            (bias, bv),
            (src, iv),
            (ft.at[:, pl.ds(pl.multiple_of(y * ROWS, ROWS), ROWS)], xbuf.at[len(PLANE)]),
            (w.at[:, pl.ds(pl.multiple_of(x * 128, 128), 128)], wbuf.at[len(PLANE)]),
        ))
    ]
    for copy in local:
        copy.start()

    pl.semaphore_wait(barrier, NX * NY - 1 + NX - 1 + 3)

    def plane_peer(i):
        dx, dy = PLANE[i]
        return up(x, NX, dx), up(y, NY, dy)

    def x_copy(i):
        xx, yy = plane_peer(i)
        rows = pl.ds(pl.multiple_of(yy * ROWS, ROWS), ROWS)
        return remote(ft.at[:, rows], xbuf.at[i], x_sem, (i,), at(xx, yy, z, c))

    def w_copy(i):
        xx, yy = plane_peer(i)
        columns = pl.ds(pl.multiple_of(xx * 128, 128), 128)
        return remote(w.at[:, columns], wbuf.at[i], w_sem, (i,), at(xx, yy, z, c))

    def w_shares(method):
        for core in range(2):

            @pl.when(c == core)
            def _():
                for i in range(core, len(PLANE), 2):
                    method(i)

    x_plane = [x_copy(i) for i in range(DIRECT)]
    for copy in x_plane[:RELAYED]:
        copy.start()
    w_shares(lambda i: w_copy(i).start())
    for copy in x_plane[RELAYED:]:
        copy.start()

    def relay(i):
        return remote(xbuf.at[i], xbuf.at[DIRECT + i], r_sem, (i,), (right, left)[i % 2])

    def s_copy(i):
        _, device = group_peer(i)
        return remote(sv.at[me], sv.at[me], s_sem, (i,), device)

    local[4].wait()
    def hand_on(i):
        return remote(wbuf.at[i], wbuf.at[i], v_sem, (i,), sibling)

    def pass_weights(i):
        w_copy(i).wait_recv()
        hand_on(i).start()

    relays = [relay(i) for i in range(RELAYED)]
    for arrival, copy in zip(x_plane, relays):
        arrival.wait_recv()
        copy.start()
    w_shares(pass_weights)
    hb[BLOCKS] = jnp.zeros((COLS, BLK), jnp.bfloat16)
    local[1].wait()
    bt[...] = jnp.broadcast_to(bv[pl.ds(x, 1), :], (128, 128)).T
    local[2].wait()
    s = iv[...]
    zz, rest = lax.shift_right_logical(s, 5), s & 31
    cc, ff = lax.shift_right_logical(rest, 4), rest & 15
    place = (zz * NY + lax.shift_right_logical(ff, 2)) * SHARD + cc * 4 + (ff & 3)
    alive = lax.broadcasted_iota(jnp.int32, s.shape, 1) < cnt[0]
    sv[me] = jnp.zeros((8, 128), jnp.int32)
    sv[me, 0:1, 0:SLOTS] = jnp.where(alive, place, BLOCKS)

    for i in range(GROUP - 1):
        s_copy(i).start()
    for core in range(2):

        @pl.when(c == core)
        def _():
            for i in range(1 - core, len(PLANE), 2):
                hand_on(i).wait_recv()

    wt[...] = wbuf[...].reshape(DEPTH, 128).T
    half = DEPTH // 2

    def transform(core, part):
        columns = wt[pl.ds(pl.multiple_of(core * COLS, COLS), COLS), part * half : (part + 1) * half]
        rows = xbuf[part * 8 : (part + 1) * 8].reshape(half, ROWS)
        return jnp.dot(columns, rows, preferred_element_type=jnp.float32)

    for copy in x_plane[RELAYED:8]:
        copy.wait_recv()
    for core in range(2):
        ht[core] = transform(core, 0)
    local[3].wait()
    for copy in x_plane[8:] + relays:
        copy.wait_recv()

    own = tiles.at[0]
    low, high = pl.ds(0, SLOTS // 2), pl.ds(SLOTS // 2, SLOTS // 2)
    t_low_right = remote(own.at[low], tbuf.at[me, low], t_sem, (0,), right)
    t_high_left = remote(own.at[high], tbuf.at[me, high], t_sem, (1,), left)
    t_high_right = remote(own.at[high], tbuf.at[me, high], t_sem, (2,), right)
    t_low_left = remote(own.at[low], tbuf.at[me, low], t_sem, (3,), left)
    t_own_sibling = remote(own, tbuf.at[me], t_sem, (4,), sibling)
    for copy in (t_low_right, t_high_left, t_high_right, t_low_left):
        copy.start()
    from_left, from_right, from_far = (down(x, NX) * 2 + c, up(x, NX) * 2 + c, up(x, NX, 2) * 2 + c)
    t_pass_right = remote(tbuf.at[from_left, low], tbuf.at[from_left, low], t_sem, (5,), right)
    t_pass_left = remote(tbuf.at[from_right, high], tbuf.at[from_right, high], t_sem, (6,), left)
    t_sibling = [
        remote(tbuf.at[e], tbuf.at[e], t_sem, (7 + j,), sibling)
        for j, e in enumerate((from_left, from_right, from_far))
    ]

    t_from_right = remote(tbuf.at[from_far, low], tbuf.at[from_far, low], t_sem, (5,), right)
    t_from_left = remote(tbuf.at[from_far, high], tbuf.at[from_far, high], t_sem, (6,), left)
    places = pltpu.make_async_copy(sv, ss, ss_sem.at[0])

    place_of = lambda zz, yy: (zz * NY + yy) * SHARD
    base = place_of(z, y) + c * 4
    other = (ht[1 - c] + transform(1 - c, 1)).astype(jnp.bfloat16)
    for k in range(4):
        stage[k] = other[:, k * BLK : (k + 1) * BLK]
    h_copy = remote(stage, hb.at[pl.ds(base, 4)], h_sem, (0,), sibling)
    h_copy.start()
    t_own_sibling.start()
    mine = (ht[c] + transform(c, 1)).astype(jnp.bfloat16)
    for k in range(4):
        hb[base + k] = mine[:, k * BLK : (k + 1) * BLK]
    h_copy.wait_recv()

    def blocks(zz, yy, first, count):
        return hb.at[pl.ds(place_of(zz, yy) + first, count)]

    def ry_copy(j):
        ref = blocks(z, y, PART, SHARD - PART)
        return remote(ref, ref, ry_sem, (j - 1,), at(x, up(y, NY, j), z, c))

    def pz_copy(zz, step, direction, first=0, count=PART):
        ref = blocks(zz, y, first, count)
        return remote(ref, ref, pz_sem, (direction, step), (above, below)[direction])

    def rz_copy(step, j, direction):
        zz = down(z, NZ, step) if direction == 0 else up(z, NZ, step)
        ref = blocks(zz, down(y, NY, j), PART, SHARD - PART)
        return remote(ref, ref, rz_sem, (direction, j, step), (above, below)[direction])

    def py_copy(zz, yy, direction):
        ref = blocks(zz, yy, 0, PART)
        return remote(ref, ref, py_sem, (direction, zz), (front, back)[direction])

    def pf_copy(zz, yy, direction, first):
        ref = blocks(zz, yy, *((0, HALF) if direction == first else (HALF, PART - HALF)))
        return remote(ref, ref, pf_sem, (direction, zz), (front, back)[direction])

    far = NZ // 2
    lower = [down(z, NZ, step) for step in range(far + 1)]
    upper = [up(z, NZ, step) for step in range(far + 1)]

    def p_copies(step):
        if step < far - 1:
            return [pz_copy(lower[step], step, 0), pz_copy(upper[step], step, 1)]
        return [pz_copy(lower[step], step, 0, 0, HALF), pz_copy(upper[step], step, 1, HALF, PART - HALF)]

    def r_copies(step, j):
        return [rz_copy(step, j, direction) for direction in range(2) if step < far - 1 or j // 2 == direction]

    def places_at(step):
        return [(lower[step], 0)] if step in (0, far) else [(lower[step], 0), (upper[step], 1)]

    def spread(step):
        for zz, _ in places_at(step):
            for direction in range(2):
                py_copy(zz, y, direction).start()

    def p_sent(step):
        for copy in p_copies(step):
            copy.wait_send()

    def r_sent(q):
        for copy in r_copies(q // NY, q % NY):
            copy.wait_send()

    def y_sent(step):
        for zz, first in places_at(step):
            for direction in range(2):
                pf_copy(zz, y, direction, first).wait_send()

    def p_step(step):
        sends = p_copies(step) if step < far else [None, None]
        for arrival, send in zip(p_copies(step - 1), sends):
            arrival.wait_recv()
            if send is not None:
                send.start()
        spread(step)
        if step >= 2:
            p_sent(step - 2)

    def r_step(q):
        step, j = q // NY, q % NY
        if step == 0 and j > 0:
            ry_copy(j).wait_recv()
        if step > 0:
            for copy in r_copies(step - 1, j):
                copy.wait_recv()
        if step < far:
            for copy in r_copies(step, j):
                copy.start()
        if q >= 8:
            r_sent(q - 8)

    def y_step(step):
        for zz, first in places_at(step):
            for direction, yy in ((0, down(y, NY)), (1, up(y, NY))):
                py_copy(zz, yy, direction).wait_recv()
                pf_copy(zz, yy, direction, first).start()
        for zz, _ in places_at(step):
            for direction in range(2):
                py_copy(zz, y, direction).wait_send()
        if step >= 2:
            y_sent(step - 2)

    def t_step(part):
        if part == 0:
            t_low_right.wait_recv()
            t_pass_right.start()
            t_high_left.wait_recv()
            t_pass_left.start()
        elif part == 1:
            t_high_right.wait_recv()
            t_sibling[0].start()
            t_low_left.wait_recv()
            t_sibling[1].start()
            for i in range(GROUP - 1):
                s_copy(i).wait_recv()
            places.start()
        else:
            t_from_right.wait_recv()
            t_from_left.wait_recv()
            t_sibling[2].start()
            local[0].wait()
            t_own_sibling.wait_recv()
            for copy in t_sibling[:2]:
                copy.wait_recv()
            places.wait()

    for j in range(1, NY):
        ry_copy(j).start()
    for copy in p_copies(0):
        copy.start()
    spread(0)
    steps = {"P": p_step, "R": r_step, "Y": y_step, "T": t_step}
    for entry in " ".join(ORDER).split():
        steps[entry[0]](int(entry[1:]))
    for j in range(NY):
        for copy in r_copies(far - 1, j):
            copy.wait_recv()

    for step in range(far + 1):
        for zz, first in places_at(step):
            for direction in range(2):
                pf_copy(zz, up(y, NY, 2), direction, first).wait_recv()

    t_sibling[2].wait_recv()

    def aggregate(e):
        total = jnp.zeros((COLS, BLK), jnp.float32)
        for first in range(0, SLOTS, UNROLL):
            slots = range(first, first + UNROLL)
            picked = jnp.concatenate([hb[ss[e, 0, t]] for t in slots], axis=1)
            values = jnp.concatenate([tbuf[e, t] for t in slots], axis=1)
            total += lax.dot_general(
                picked, values, (((1,), (1,)), ((), ())), preferred_element_type=jnp.float32
            )
        return jnp.maximum(total + bt[pl.ds(pl.multiple_of(c * COLS, COLS), COLS), :], 0.0).astype(jnp.bfloat16)

    def o_copy(i):
        _, device = group_peer(i)
        return remote(obuf.at[i], rbuf.at[me], o_sem, (i,), device)

    @pl.loop(0, GROUP - 1)
    def _(i):
        e, _ = group_peer(i)
        obuf[i] = aggregate(e)
        o_copy(i).start()

    rbuf[me] = aggregate(me)

    for copy in x_plane + relays:
        copy.wait_send()

    def w_over(i):
        w_copy(i).wait_send()
        hand_on(i).wait_send()

    w_shares(w_over)

    for i in range(GROUP - 1):
        s_copy(i).wait_send()
    for copy in (t_low_right, t_high_left, t_high_right, t_low_left, t_own_sibling, t_pass_right, t_pass_left, h_copy):
        copy.wait_send()
    for copy in t_sibling:
        copy.wait_send()
    for j in range(1, NY):
        ry_copy(j).wait_send()

    p_sent(far - 1)
    for q in range(NY * far - 8, NY * far):
        r_sent(q)
    for step in (far - 1, far):
        y_sent(step)

    @pl.loop(0, GROUP - 1)
    def _(i):
        o_copy(i).wait_recv()

    out[...] = rbuf[...].reshape(GROUP * COLS, BLK).T

    @pl.loop(0, GROUP - 1)
    def _(i):
        o_copy(i).wait_send()


def shards(features, weight, bias, tile_src, tile_count, tile_vals):
    rows, depth = features.shape
    vmem = pl.BlockSpec(memory_space=pltpu.VMEM)
    hbm = pl.BlockSpec(memory_space=pltpu.HBM)
    smem = pl.BlockSpec(memory_space=pltpu.SMEM)
    dma = pltpu.SemaphoreType.DMA
    bf16 = jnp.bfloat16
    return pl.pallas_call(
        kernel,
        out_shape=jax.ShapeDtypeStruct((BLK, GROUP * COLS), bf16),
        in_specs=[hbm, hbm, hbm, hbm, smem, hbm],
        out_specs=vmem,
        scratch_shapes=[
            pltpu.VMEM((NX * NY, depth, rows // NY), bf16),
            pltpu.VMEM((NX * NY, depth, 128), bf16),
            pltpu.VMEM((BLOCKS + 1, COLS, BLK), bf16),
            pltpu.VMEM((4, COLS, BLK), bf16),
            pltpu.VMEM((GROUP, SLOTS, BLK, BLK), bf16),
            pltpu.VMEM((GROUP, 8, 128), jnp.int32),
            pltpu.SMEM((GROUP, 8, 128), jnp.int32),
            pltpu.VMEM((128, 128), jnp.float32),
            pltpu.VMEM((GROUP, COLS, BLK), bf16),
            pltpu.VMEM((GROUP, COLS, BLK), bf16),
            pltpu.VMEM((NX, 128), jnp.float32),
            pltpu.VMEM((1, SLOTS), jnp.int32),
            pltpu.VMEM((128, DEPTH), bf16),
            pltpu.VMEM((2, COLS, ROWS), jnp.float32),
            dma((2, RELAYED)),
            dma((2, NX * NY - 1)),
            dma((2, NX * NY - 1)),
            dma((2, NX * NY - 1)),
            dma((2, GROUP - 1)),
            dma((1,)),
            dma((2, 10)),
            dma((5,)),
            dma((2, 1)),
            dma((2, NY - 1)),
            dma((2, 2, NZ // 2)),
            dma((2, 2, NY, NZ // 2)),
            dma((2, 2, NZ)),
            dma((2, 2, NZ)),
            dma((2, GROUP - 1)),
        ],
        compiler_params=pltpu.CompilerParams(
            collective_id=0, has_side_effects=True, vmem_limit_bytes=56 * 2**20
        ),
    )(features.T, weight, bias.reshape(NX, 128), tile_src, tile_count, tile_vals)


def solution(mesh):
    placed = (
        P("node", "feat"),
        P("feat", None),
        P(),
        P(("node", "feat"), None),
        P(("node", "feat")),
        P(("node", "feat"), None, None, None),
    )
    return jax.shard_map(
        shards, mesh=mesh, in_specs=placed, out_specs=P(("node", "feat"), None), check_vma=False
    )
```

```python
import jax
import jax.numpy as jnp
from jax import lax
from jax.experimental import pallas as pl
from jax.experimental.pallas import tpu as pltpu
from jax.sharding import PartitionSpec as P

MESH = pl.DeviceIdType.MESH
NX, NY, NZ = 4, 4, 16
BLK = 128
COLS = 64
GROUP = 2 * NX
PART = 5
SHARD = 8
HALF = 3
BLOCKS = NZ * NY * SHARD
SLOTS = 32
UNROLL = 32
ROWS = 512
DEPTH = 768
DIRECT, RELAYED = 11, 4
ORDER = (
    "R0 R1 P1 R2", "Y0 R3 R4 P2", "R5 Y1 R6 R7", "P3 R8 Y2 R9",
    "R10 P4 R11 R12", "Y3 R13 P5 T0", "R14 R15 Y4 R16", "P6 R17 R18 Y5",
    "R19 P7 T1 R20", "R21 R22 P8 R23", "R24 Y6 R25 R26", "T2 Y7 R27 Y8",
    "R28 R30 R29 R31",
)
PLANE = (
    (1, 0), (3, 3), (1, 1), (3, 2), (1, 2), (3, 0), (1, 3), (3, 1), (0, 2), (0, 1), (0, 3), (2, 0), (2, 3), (2, 1), (2, 2),
)


def kernel(
    ft, w, bias, src, cnt, tiles, out,
    xbuf, wbuf, hb, stage, tbuf, sv, ss, bt, obuf, rbuf,
    bv, iv, wt, ht, r_sem, x_sem, w_sem, v_sem, s_sem, ss_sem, t_sem, local_sem, h_sem, ry_sem, pz_sem, rz_sem, py_sem, pf_sem, o_sem,
):
    n = lax.axis_index("node")
    f = lax.axis_index("feat")
    z, c = lax.div(n, 2), lax.rem(n, 2)
    x, y = lax.div(f, NY), lax.rem(f, NY)
    me = x * 2 + c

    def at(xx, yy, zz, cc):
        return (zz * 2 + cc, xx * NY + yy)

    def up(value, size, by=1):
        return lax.rem(value + by, size)

    def down(value, size, by=1):
        return lax.rem(value + size - by, size)

    def remote(source, target, sems, index, device):
        return pltpu.make_async_remote_copy(
            src_ref=source, dst_ref=target, send_sem=sems.at[(0,) + index], recv_sem=sems.at[(1,) + index],
            device_id=device, device_id_type=MESH,
        )

    sibling = at(x, y, z, 1 - c)
    right, left = at(up(x, NX), y, z, c), at(down(x, NX), y, z, c)
    front, back = at(x, up(y, NY), z, c), at(x, down(y, NY), z, c)
    above, below = at(x, y, up(z, NZ), c), at(x, y, down(z, NZ), c)

    def group_offset(i):
        k = lax.div(i, 2)
        return lax.rem(2 + 3 * k + 3 * lax.div(k * (k - 1), 2), NX), 1 - lax.rem(i, 2)

    def group_peer(i):
        dx, dc = group_offset(i)
        xx, cc = up(x, NX, dx), lax.rem(c + dc, 2)
        return xx * 2 + cc, at(xx, y, z, cc)

    def group_source(i):
        dx, dc = group_offset(i)
        return down(x, NX, dx) * 2 + lax.rem(c + dc, 2)

    barrier = pltpu.get_barrier_semaphore()

    @pl.loop(1, NX * NY)
    def _(i):
        pl.semaphore_signal(barrier, inc=1, device_id=(n, lax.rem(f + i, NX * NY)), device_id_type=MESH)

    for i in range(1, NX):
        pl.semaphore_signal(barrier, inc=1, device_id=at(up(x, NX, i), y, z, 1 - c), device_id_type=MESH)
    for device in (sibling, above, below):
        pl.semaphore_signal(barrier, inc=1, device_id=device, device_id_type=MESH)

    local = [
        pltpu.make_async_copy(source, target, local_sem.at[i])
        for i, (source, target) in enumerate((
            (tiles.at[0], tbuf.at[me]),
            (bias, bv),
            (src, iv),
            (ft.at[:, pl.ds(pl.multiple_of(y * ROWS, ROWS), ROWS)], xbuf.at[len(PLANE)]),
            (w.at[:, pl.ds(pl.multiple_of(x * 128, 128), 128)], wbuf.at[len(PLANE)]),
        ))
    ]
    for copy in local:
        copy.start()

    pl.semaphore_wait(barrier, NX * NY - 1 + NX - 1 + 3)

    def plane_peer(i):
        dx, dy = PLANE[i]
        return up(x, NX, dx), up(y, NY, dy)

    def x_copy(i):
        xx, yy = plane_peer(i)
        rows = pl.ds(pl.multiple_of(yy * ROWS, ROWS), ROWS)
        return remote(ft.at[:, rows], xbuf.at[i], x_sem, (i,), at(xx, yy, z, c))

    def w_copy(i):
        xx, yy = plane_peer(i)
        columns = pl.ds(pl.multiple_of(xx * 128, 128), 128)
        return remote(w.at[:, columns], wbuf.at[i], w_sem, (i,), at(xx, yy, z, c))

    def w_shares(method):
        for core in range(2):

            @pl.when(c == core)
            def _():
                for i in range(core, len(PLANE), 2):
                    method(i)

    x_plane = [x_copy(i) for i in range(DIRECT)]
    for copy in x_plane[:RELAYED]:
        copy.start()
    w_shares(lambda i: w_copy(i).start())
    for copy in x_plane[RELAYED:]:
        copy.start()

    def relay(i):
        return remote(xbuf.at[i], xbuf.at[DIRECT + i], r_sem, (i,), (right, left)[i % 2])

    def s_copy(i):
        _, device = group_peer(i)
        return remote(sv.at[me], sv.at[me], s_sem, (i,), device)

    local[4].wait()
    def hand_on(i):
        return remote(wbuf.at[i], wbuf.at[i], v_sem, (i,), sibling)

    def pass_weights(i):
        w_copy(i).wait_recv()
        hand_on(i).start()

    relays = [relay(i) for i in range(RELAYED)]
    for arrival, copy in zip(x_plane, relays):
        arrival.wait_recv()
        copy.start()
    w_shares(pass_weights)
    hb[BLOCKS] = jnp.zeros((COLS, BLK), jnp.bfloat16)
    local[1].wait()
    bt[...] = jnp.broadcast_to(bv[pl.ds(x, 1), :], (128, 128)).T
    local[2].wait()
    s = iv[...]
    zz, rest = lax.shift_right_logical(s, 5), s & 31
    cc, ff = lax.shift_right_logical(rest, 4), rest & 15
    place = (zz * NY + lax.shift_right_logical(ff, 2)) * SHARD + cc * 4 + (ff & 3)
    alive = lax.broadcasted_iota(jnp.int32, s.shape, 1) < cnt[0]
    sv[me] = jnp.zeros((8, 128), jnp.int32)
    sv[me, 0:1, 0:SLOTS] = jnp.where(alive, place, BLOCKS)

    for i in range(GROUP - 1):
        s_copy(i).start()
    for core in range(2):

        @pl.when(c == core)
        def _():
            for i in range(1 - core, len(PLANE), 2):
                hand_on(i).wait_recv()

    wt[...] = wbuf[...].reshape(DEPTH, 128).T
    half = DEPTH // 2

    def transform(core, part):
        columns = wt[pl.ds(pl.multiple_of(core * COLS, COLS), COLS), part * half : (part + 1) * half]
        rows = xbuf[part * 8 : (part + 1) * 8].reshape(half, ROWS)
        return jnp.dot(columns, rows, preferred_element_type=jnp.float32)

    for copy in x_plane[RELAYED:8]:
        copy.wait_recv()
    for core in range(2):
        ht[core] = transform(core, 0)
    local[3].wait()
    for copy in x_plane[8:] + relays:
        copy.wait_recv()

    own = tiles.at[0]
    low, high = pl.ds(0, SLOTS // 2), pl.ds(SLOTS // 2, SLOTS // 2)
    t_low_right = remote(own.at[low], tbuf.at[me, low], t_sem, (0,), right)
    t_high_left = remote(own.at[high], tbuf.at[me, high], t_sem, (1,), left)
    t_high_right = remote(own.at[high], tbuf.at[me, high], t_sem, (2,), right)
    t_low_left = remote(own.at[low], tbuf.at[me, low], t_sem, (3,), left)
    t_own_sibling = remote(own, tbuf.at[me], t_sem, (4,), sibling)
    for copy in (t_low_right, t_high_left, t_high_right, t_low_left):
        copy.start()
    from_left, from_right, from_far = (down(x, NX) * 2 + c, up(x, NX) * 2 + c, up(x, NX, 2) * 2 + c)
    t_pass_right = remote(tbuf.at[from_left, low], tbuf.at[from_left, low], t_sem, (5,), right)
    t_pass_left = remote(tbuf.at[from_right, high], tbuf.at[from_right, high], t_sem, (6,), left)
    t_sibling = [
        remote(tbuf.at[e], tbuf.at[e], t_sem, (7 + j,), sibling)
        for j, e in enumerate((from_left, from_right, from_far))
    ]

    t_from_right = remote(tbuf.at[from_far, low], tbuf.at[from_far, low], t_sem, (5,), right)
    t_from_left = remote(tbuf.at[from_far, high], tbuf.at[from_far, high], t_sem, (6,), left)
    places = pltpu.make_async_copy(sv, ss, ss_sem.at[0])

    place_of = lambda zz, yy: (zz * NY + yy) * SHARD
    base = place_of(z, y) + c * 4
    other = (ht[1 - c] + transform(1 - c, 1)).astype(jnp.bfloat16)
    for k in range(4):
        stage[k] = other[:, k * BLK : (k + 1) * BLK]
    h_copy = remote(stage, hb.at[pl.ds(base, 4)], h_sem, (0,), sibling)
    h_copy.start()
    t_own_sibling.start()
    mine = (ht[c] + transform(c, 1)).astype(jnp.bfloat16)
    for k in range(4):
        hb[base + k] = mine[:, k * BLK : (k + 1) * BLK]
    h_copy.wait_recv()

    def blocks(zz, yy, first, count):
        return hb.at[pl.ds(place_of(zz, yy) + first, count)]

    def ry_copy(j):
        ref = blocks(z, y, PART, SHARD - PART)
        return remote(ref, ref, ry_sem, (j - 1,), at(x, up(y, NY, j), z, c))

    def pz_copy(zz, step, direction, first=0, count=PART):
        ref = blocks(zz, y, first, count)
        return remote(ref, ref, pz_sem, (direction, step), (above, below)[direction])

    def rz_copy(step, j, direction):
        zz = down(z, NZ, step) if direction == 0 else up(z, NZ, step)
        ref = blocks(zz, down(y, NY, j), PART, SHARD - PART)
        return remote(ref, ref, rz_sem, (direction, j, step), (above, below)[direction])

    def py_copy(zz, yy, direction):
        ref = blocks(zz, yy, 0, PART)
        return remote(ref, ref, py_sem, (direction, zz), (front, back)[direction])

    def pf_copy(zz, yy, direction, first):
        ref = blocks(zz, yy, *((0, HALF) if direction == first else (HALF, PART - HALF)))
        return remote(ref, ref, pf_sem, (direction, zz), (front, back)[direction])

    far = NZ // 2
    lower = [down(z, NZ, step) for step in range(far + 1)]
    upper = [up(z, NZ, step) for step in range(far + 1)]

    def p_copies(step):
        if step < far - 1:
            return [pz_copy(lower[step], step, 0), pz_copy(upper[step], step, 1)]
        return [pz_copy(lower[step], step, 0, 0, HALF), pz_copy(upper[step], step, 1, HALF, PART - HALF)]

    def r_copies(step, j):
        return [rz_copy(step, j, direction) for direction in range(2) if step < far - 1 or j // 2 == direction]

    def places_at(step):
        return [(lower[step], 0)] if step in (0, far) else [(lower[step], 0), (upper[step], 1)]

    def spread(step):
        for zz, _ in places_at(step):
            for direction in range(2):
                py_copy(zz, y, direction).start()

    def p_sent(step):
        for copy in p_copies(step):
            copy.wait_send()

    def r_sent(q):
        for copy in r_copies(q // NY, q % NY):
            copy.wait_send()

    def y_sent(step):
        for zz, first in places_at(step):
            for direction in range(2):
                pf_copy(zz, y, direction, first).wait_send()

    def p_step(step):
        sends = p_copies(step) if step < far else [None, None]
        for arrival, send in zip(p_copies(step - 1), sends):
            arrival.wait_recv()
            if send is not None:
                send.start()
        spread(step)
        if step >= 2:
            p_sent(step - 2)

    def r_step(q):
        step, j = q // NY, q % NY
        if step == 0 and j > 0:
            ry_copy(j).wait_recv()
        if step > 0:
            for copy in r_copies(step - 1, j):
                copy.wait_recv()
        if step < far:
            for copy in r_copies(step, j):
                copy.start()
        if q >= 8:
            r_sent(q - 8)

    def y_step(step):
        for zz, first in places_at(step):
            for direction, yy in ((0, down(y, NY)), (1, up(y, NY))):
                py_copy(zz, yy, direction).wait_recv()
                pf_copy(zz, yy, direction, first).start()
        for zz, _ in places_at(step):
            for direction in range(2):
                py_copy(zz, y, direction).wait_send()
        if step >= 2:
            y_sent(step - 2)

    def t_step(part):
        if part == 0:
            t_low_right.wait_recv()
            t_pass_right.start()
            t_high_left.wait_recv()
            t_pass_left.start()
        elif part == 1:
            t_high_right.wait_recv()
            t_sibling[0].start()
            t_low_left.wait_recv()
            t_sibling[1].start()
            for i in range(GROUP - 1):
                s_copy(i).wait_recv()
            places.start()
        else:
            t_from_right.wait_recv()
            t_from_left.wait_recv()
            t_sibling[2].start()
            local[0].wait()
            t_own_sibling.wait_recv()
            for copy in t_sibling[:2]:
                copy.wait_recv()
            places.wait()

    for j in range(1, NY):
        ry_copy(j).start()
    for copy in p_copies(0):
        copy.start()
    spread(0)
    steps = {"P": p_step, "R": r_step, "Y": y_step, "T": t_step}
    for entry in " ".join(ORDER).split():
        steps[entry[0]](int(entry[1:]))
    for j in range(NY):
        for copy in r_copies(far - 1, j):
            copy.wait_recv()

    for step in range(far + 1):
        for zz, first in places_at(step):
            for direction in range(2):
                pf_copy(zz, up(y, NY, 2), direction, first).wait_recv()

    t_sibling[2].wait_recv()

    def aggregate(e):
        total = jnp.zeros((COLS, BLK), jnp.float32)
        for first in range(0, SLOTS, UNROLL):
            slots = range(first, first + UNROLL)
            picked = jnp.concatenate([hb[ss[e, 0, t]] for t in slots], axis=1)
            values = jnp.concatenate([tbuf[e, t] for t in slots], axis=1)
            total += lax.dot_general(
                picked, values, (((1,), (1,)), ((), ())), preferred_element_type=jnp.float32
            )
        return jnp.maximum(total + bt[pl.ds(pl.multiple_of(c * COLS, COLS), COLS), :], 0.0).astype(jnp.bfloat16)

    def o_copy(i):
        _, device = group_peer(i)
        return remote(obuf.at[i], rbuf.at[me], o_sem, (i,), device)

    @pl.loop(0, GROUP - 1)
    def _(i):
        e, _ = group_peer(i)
        obuf[i] = aggregate(e)
        o_copy(i).start()

    rbuf[me] = aggregate(me)

    for copy in x_plane + relays:
        copy.wait_send()

    def w_over(i):
        w_copy(i).wait_send()
        hand_on(i).wait_send()

    w_shares(w_over)

    for i in range(GROUP - 1):
        s_copy(i).wait_send()
    for copy in (t_low_right, t_high_left, t_high_right, t_low_left, t_own_sibling, t_pass_right, t_pass_left, h_copy):
        copy.wait_send()
    for copy in t_sibling:
        copy.wait_send()
    for j in range(1, NY):
        ry_copy(j).wait_send()

    p_sent(far - 1)
    for q in range(NY * far - 8, NY * far):
        r_sent(q)
    for step in (far - 1, far):
        y_sent(step)

    @pl.loop(0, GROUP - 1)
    def _(i):
        o_copy(i).wait_recv()

    out[...] = rbuf[...].reshape(GROUP * COLS, BLK).T

    @pl.loop(0, GROUP - 1)
    def _(i):
        o_copy(i).wait_send()


def shards(features, weight, bias, tile_src, tile_count, tile_vals):
    rows, depth = features.shape
    vmem = pl.BlockSpec(memory_space=pltpu.VMEM)
    hbm = pl.BlockSpec(memory_space=pltpu.HBM)
    smem = pl.BlockSpec(memory_space=pltpu.SMEM)
    dma = pltpu.SemaphoreType.DMA
    bf16 = jnp.bfloat16
    return pl.pallas_call(
        kernel,
        out_shape=jax.ShapeDtypeStruct((BLK, GROUP * COLS), bf16),
        in_specs=[hbm, hbm, hbm, hbm, smem, hbm],
        out_specs=vmem,
        scratch_shapes=[
            pltpu.VMEM((NX * NY, depth, rows // NY), bf16),
            pltpu.VMEM((NX * NY, depth, 128), bf16),
            pltpu.VMEM((BLOCKS + 1, COLS, BLK), bf16),
            pltpu.VMEM((4, COLS, BLK), bf16),
            pltpu.VMEM((GROUP, SLOTS, BLK, BLK), bf16),
            pltpu.VMEM((GROUP, 8, 128), jnp.int32),
            pltpu.SMEM((GROUP, 8, 128), jnp.int32),
            pltpu.VMEM((128, 128), jnp.float32),
            pltpu.VMEM((GROUP, COLS, BLK), bf16),
            pltpu.VMEM((GROUP, COLS, BLK), bf16),
            pltpu.VMEM((NX, 128), jnp.float32),
            pltpu.VMEM((1, SLOTS), jnp.int32),
            pltpu.VMEM((128, DEPTH), bf16),
            pltpu.VMEM((2, COLS, ROWS), jnp.float32),
            dma((2, RELAYED)),
            dma((2, NX * NY - 1)),
            dma((2, NX * NY - 1)),
            dma((2, NX * NY - 1)),
            dma((2, GROUP - 1)),
            dma((1,)),
            dma((2, 10)),
            dma((5,)),
            dma((2, 1)),
            dma((2, NY - 1)),
            dma((2, 2, NZ // 2)),
            dma((2, 2, NY, NZ // 2)),
            dma((2, 2, NZ)),
            dma((2, 2, NZ)),
            dma((2, GROUP - 1)),
        ],
        compiler_params=pltpu.CompilerParams(
            collective_id=0, has_side_effects=True, vmem_limit_bytes=56 * 2**20
        ),
    )(features.T, weight, bias.reshape(NX, 128), tile_src, tile_count, tile_vals)


def solution(mesh):
    placed = (
        P("node", "feat"),
        P("feat", None),
        P(),
        P(("node", "feat"), None),
        P(("node", "feat")),
        P(("node", "feat"), None, None, None),
    )
    return jax.shard_map(
        shards, mesh=mesh, in_specs=placed, out_specs=P(("node", "feat"), None), check_vma=False
    )
```
